512 devices in a mesh: rep: 64 (over z, x), tp: 8 (over y, core).
Axes of the slice: x: 4, y: 4, z: 16, core: 2. Of those that a mesh axis runs over, the one named last changes fastest.
Arguments:
- grads: bfloat16 [2, 64, 14336, 128], P(None, 'rep', 'tp'), may hold values from -6 to 6
- error_in: float32 [64, 14336, 128], P('rep', 'tp'), may hold values from -6 to 6
- accum_in: float32 [14336, 128], P('tp'), may hold values from -6 to 6
- picks: int32 [2, 64, 8, 2], P(None, None, 'tp'), may hold values from 0 to 1791, as said below
Outputs:
- accum_out: float32 [14336, 128], P('tp')
- error_out: float32 [64, 14336, 128], P('rep', 'tp')
The draws below stay inside these ranges and needn't reach their ends.
Inputs may be any that keep to these rules, and one draw needn't show every extreme that they name: Each row picks[s, r, t, :] holds 2 different block numbers.
All inputs are finite; a program needn't handle non-finite values.
Results may differ from the reference program's by a relative error of at most 0.0003.
Values sent between devices are 32-bit elements; how exact they have to be, the bound alone decides.
No kernel may reach another device: no remote copies, remote signals or barrier semaphores. Data moves between devices by JAX's collectives and lax.ppermute only.
A program may use at most 64 MiB of HBM per device.

```python
import jax
import jax.numpy as jnp

BLOCK = 128
NB_DEV = 1792
STEPS = 2
NB = 14336
N_REP = 64
N_TP = 8


def draw_picks(key, part):
    key = jax.random.fold_in(key, 1)
    key_first, key_gap, key_holder = jax.random.split(key, 3)
    first_pick = jax.random.randint(key_first, (STEPS, N_REP, N_TP), 0, NB_DEV, dtype=jnp.int32)
    gap_size = jax.random.randint(key_gap, (STEPS, N_REP, N_TP), 1, NB_DEV, dtype=jnp.int32)
    second_pick = (first_pick + gap_size) % NB_DEV
    holder = jax.random.randint(key_holder, (STEPS, 1, N_TP), 0, N_REP, dtype=jnp.int32)
    replicas = jnp.arange(N_REP, dtype=jnp.int32)[None, :, None]
    marked = replicas == holder
    first_pick = jnp.where(marked, jnp.int32(NB_DEV - 1), first_pick)
    second_pick = jnp.where(marked, jnp.int32(0), second_pick)
    return jnp.stack([first_pick, second_pick], axis=-1).astype(jnp.int32)


def levels(stream_key, dims, shards, low, top_value):
    def one(position, shards_of):
        draws = jax.random.uniform(jax.random.fold_in(jax.random.fold_in(stream_key, 6), position), (shards_of,), jnp.float32, low / len(shards), top_value / len(shards))
        return jnp.repeat(jnp.exp(draws), dims[position] // shards_of).reshape((-1,) + (1,) * (len(dims) - position - 1))

    factor_of = one(*shards[0])
    for cut in shards[1:]:
        factor_of = factor_of * one(*cut)
    return factor_of


def normal_values(stream_key, shape, deviation, reach, shards=(), kind=jnp.bfloat16):
    array = deviation * jax.random.normal(stream_key, shape, jnp.float32)
    if shards:
        array = array * levels(stream_key, shape, shards, -0.22, 0.18)
    return jnp.clip(array, -reach, reach).astype(kind)


def setup_inputs(seed: int = 0) -> dict:
    seeds = jax.random.split(jax.random.key(seed), 5)
    return {
        "grads": normal_values(seeds[0], (STEPS, N_REP, NB, BLOCK), 1.0, 6.0, ((1, 64), (2, 8))),
        "error_in": normal_values(seeds[1], (N_REP, NB, BLOCK), 1.0, 6.0, ((0, 64), (1, 8)), jnp.float32),
        "accum_in": normal_values(seeds[2], (NB, BLOCK), 1.0, 6.0, ((0, 8),), jnp.float32),
        "picks": draw_picks(jax.random.fold_in(seeds[4], 71), 0),
    }


def reference(grads, error_in, accum_in, picks):
    error = error_in
    accum = accum_in
    positions = jnp.arange(NB_DEV, dtype=jnp.int32)
    for step in range(STEPS):
        corrected = grads[step].astype(jnp.float32) + error
        chosen = jnp.any(picks[step][:, :, :, None] == positions[None, None, None, :], axis=2)
        chosen = chosen.reshape(N_REP, NB)
        sent = jnp.where(chosen[:, :, None], corrected, jnp.float32(0.0))
        accum = accum + jnp.sum(sent, axis=0)
        error = corrected - sent
    return accum, error
```

```python
import functools

import jax
import jax.numpy as jnp
from jax import lax
from jax.experimental import pallas as pl
from jax.experimental.pallas import tpu as pltpu
from jax.sharding import PartitionSpec as P

STEPS = 2
PICKS = 2
BLOCK = 128
SENT = STEPS * PICKS
FIRST = 39
F_ROWS = 8
H_ROWS = 16
KIB = 1024
ROOM = 12 * 1024 * KIB
NEARLY_ALL = (63 * 1024 + 256) * KIB


def kernel_params(limit=ROOM):
    return pltpu.CompilerParams(vmem_limit_bytes=limit)


def send_kernel(picks, grads, error, rows, halves, wholes, half_sems, whole_sems):
    replica = lax.axis_index("rep")
    chosen = [picks[j // PICKS, j % PICKS, replica] for j in range(SENT)]
    copies = []
    for j in range(SENT):
        base = pl.multiple_of((chosen[j] // F_ROWS) * F_ROWS, F_ROWS)
        copies.append(
            pltpu.make_async_copy(
                error.at[0, pl.ds(base, F_ROWS), :], wholes.at[j], whole_sems.at[j]
            )
        )
        base = pl.multiple_of((chosen[j] // H_ROWS) * H_ROWS, H_ROWS)
        for step in range(j // PICKS + 1):
            copies.append(
                pltpu.make_async_copy(
                    grads.at[step, 0, pl.ds(base, H_ROWS), :],
                    halves.at[step, j],
                    half_sems.at[step, j],
                )
            )
    for copy in copies:
        copy.start()
    for copy in copies:
        copy.wait()

    def row_of(tile, at):
        index = lax.broadcasted_iota(jnp.int32, tile.shape, 0)
        kept = jnp.where(index == at, tile, jnp.float32(0.0))
        return jnp.sum(kept, axis=0, keepdims=True)

    sent = []
    for j in range(SENT):
        at = lax.rem(chosen[j], H_ROWS)
        value = row_of(halves[0, j].astype(jnp.float32), at)
        value = value + row_of(wholes[j], lax.rem(chosen[j], F_ROWS))
        if j >= PICKS:
            again = (chosen[j] == chosen[0]) | (chosen[j] == chosen[1])
            value = jnp.where(again, jnp.float32(0.0), value)
            value = row_of(halves[1, j].astype(jnp.float32), at) + value
        sent.append(value)
    block = jnp.concatenate(sent, axis=0)
    for peer in range(rows.shape[0]):
        rows[peer] = block


def sent_rows(picks, grads, error, copies):
    return pl.pallas_call(
        send_kernel,
        out_shape=jax.ShapeDtypeStruct((copies, SENT, BLOCK), jnp.float32),
        in_specs=[
            pl.BlockSpec(memory_space=pltpu.SMEM),
            pl.BlockSpec(memory_space=pltpu.HBM),
            pl.BlockSpec(memory_space=pltpu.HBM),
        ],
        out_specs=pl.BlockSpec(memory_space=pltpu.VMEM),
        scratch_shapes=[
            pltpu.VMEM((STEPS, SENT, H_ROWS, BLOCK), jnp.bfloat16),
            pltpu.VMEM((SENT, F_ROWS, BLOCK), jnp.float32),
            pltpu.SemaphoreType.DMA((STEPS, SENT)),
            pltpu.SemaphoreType.DMA((SENT,)),
        ],
        compiler_params=kernel_params(NEARLY_ALL),
        name="sent_rows",
    )(picks, grads, error)


def error_kernel(head, picks, table, grads, error, out, hot):
    replica = lax.axis_index("rep")
    size = out.shape[1]
    first = pl.program_id(0) * size
    index = lax.broadcasted_iota(jnp.int32, (size, BLOCK), 0) + first
    value = error[0]
    for step in range(STEPS):
        value = grads[step, 0].astype(jnp.float32) + value
        for k in range(PICKS):
            value = jnp.where(index == picks[step, k, replica], jnp.float32(0.0), value)
    out[0] = value
    lanes = []
    for j in range(SENT):
        lane = table[j // PICKS, pl.ds(j % PICKS, 1), :]
        lanes += [lane[:, head:], lane[:, :head]]
    order = jnp.concatenate(lanes, axis=1)
    index = lax.broadcasted_iota(jnp.int32, hot.shape, 0) + first
    hits = jnp.where(index == order, jnp.float32(1.0), jnp.float32(0.0))
    hot[...] = hits.astype(jnp.bfloat16)


def next_error(head, picks, grads, error, tiles=4):
    blocks = error.shape[1]
    size = blocks // tiles
    count = SENT * picks.shape[2]
    return pl.pallas_call(
        functools.partial(error_kernel, head),
        grid=(tiles,),
        out_shape=(
            jax.ShapeDtypeStruct(error.shape, jnp.float32),
            jax.ShapeDtypeStruct((blocks, count), jnp.bfloat16),
        ),
        in_specs=[
            pl.BlockSpec(memory_space=pltpu.SMEM),
            pl.BlockSpec(picks.shape, lambda i: (0, 0, 0)),
            pl.BlockSpec((STEPS, 1, size, BLOCK), lambda i: (0, 0, i, 0)),
            pl.BlockSpec((1, size, BLOCK), lambda i: (0, i, 0)),
        ],
        out_specs=(
            pl.BlockSpec((1, size, BLOCK), lambda i: (0, i, 0)),
            pl.BlockSpec((size, count), lambda i: (i, 0)),
        ),
        compiler_params=kernel_params(),
        cost_estimate=pl.CostEstimate(
            flops=8 * error.size, bytes_accessed=16 * error.size, transcendentals=0
        ),
        name="next_error",
    )(picks, picks, grads, error)


def add_kernel(hot, rows, accum, out, sums, sems):
    count = rows.shape[0] // SENT
    value = jnp.concatenate(
        [rows[pl.ds(j, count, SENT), :] for j in range(SENT)], axis=0
    )
    high = value.astype(jnp.bfloat16)
    rest = value - high.astype(jnp.float32)
    middle = rest.astype(jnp.bfloat16)
    low = (rest - middle.astype(jnp.float32)).astype(jnp.bfloat16)
    pair = jnp.concatenate([high, middle], axis=1)
    tiles = sems.shape[0]
    size = accum.shape[0] // tiles
    copies = []
    for tile in range(tiles):
        part = pl.ds(tile * size, size)
        both = jnp.dot(hot[part, :], pair, preferred_element_type=jnp.float32)
        small = jnp.dot(hot[part, :], low, preferred_element_type=jnp.float32)
        total = both[:, :BLOCK] + (both[:, BLOCK:] + small)
        sums[part, :] = accum[part, :] + total
        copy = pltpu.make_async_copy(sums.at[part, :], out.at[part, :], sems.at[tile])
        copy.start()
        copies.append(copy)
    for copy in copies:
        copy.wait()


def add_rows(hot, rows, accum, tiles=7):
    return pl.pallas_call(
        add_kernel,
        out_shape=jax.ShapeDtypeStruct(accum.shape, jnp.float32),
        in_specs=[pl.BlockSpec(memory_space=pltpu.VMEM)] * 3,
        out_specs=pl.BlockSpec(memory_space=pltpu.HBM),
        scratch_shapes=[
            pltpu.VMEM(accum.shape, jnp.float32),
            pltpu.SemaphoreType.DMA((tiles,)),
        ],
        compiler_params=kernel_params(),
        name="add_rows",
    )(hot, rows, accum)


def local(grads, error_in, accum_in, picks):
    table = jnp.swapaxes(picks[:, :, 0, :], 1, 2)
    count = lax.axis_size("rep")
    first = FIRST
    members = [(first + r) % count for r in range(count)]
    rows = sent_rows(table, grads, error_in, count)
    rows = lax.all_to_all(
        rows, "rep", 0, 0, axis_index_groups=[members], tiled=True
    )
    error, hot = next_error(first, table, grads, error_in)
    rows = rows.reshape(count * SENT, BLOCK)
    return (add_rows(hot, rows, accum_in), error)


def solution(mesh):
    placed = (
        P(None, "rep", "tp", None),
        P("rep", "tp", None),
        P("tp", None),
        P(None, None, "tp", None),
    )
    return jax.shard_map(
        local,
        mesh=mesh,
        in_specs=placed,
        out_specs=(P("tp", None), P("rep", "tp", None)),
        check_vma=False,
    )
```

```python
import functools

import jax
import jax.numpy as jnp
from jax import lax
from jax.experimental import pallas as pl
from jax.experimental.pallas import tpu as pltpu
from jax.sharding import PartitionSpec as P

STEPS = 2
PICKS = 2
BLOCK = 128
SENT = STEPS * PICKS
WIDE = 4
FIRST_Z = 9
FIRST_X = 3
EARLY_Z = 1
F_ROWS = 8
H_ROWS = 16
KIB = 1024
ROOM = 12 * 1024 * KIB
NEARLY_ALL = (63 * 1024 + 256) * KIB


def kernel_params(limit=ROOM):
    return pltpu.CompilerParams(vmem_limit_bytes=limit)


def send_kernel(picks, grads, error, rows, halves, wholes, half_sems, whole_sems):
    replica = lax.axis_index("rep")
    chosen = [picks[j // PICKS, j % PICKS, replica] for j in range(SENT)]
    copies = []
    for j in range(SENT):
        base = pl.multiple_of((chosen[j] // F_ROWS) * F_ROWS, F_ROWS)
        copies.append(
            pltpu.make_async_copy(
                error.at[0, pl.ds(base, F_ROWS), :], wholes.at[j], whole_sems.at[j]
            )
        )
        base = pl.multiple_of((chosen[j] // H_ROWS) * H_ROWS, H_ROWS)
        steps = pl.ds(0, j // PICKS + 1)
        copies.append(
            pltpu.make_async_copy(
                grads.at[steps, 0, pl.ds(base, H_ROWS), :],
                halves.at[j, steps],
                half_sems.at[j],
            )
        )
    for copy in copies:
        copy.start()
    for copy in copies:
        copy.wait()

    def row_of(tile, at):
        index = lax.broadcasted_iota(jnp.int32, tile.shape, 0)
        kept = jnp.where(index == at, tile, jnp.float32(0.0))
        return jnp.sum(kept, axis=0, keepdims=True)

    sent = []
    for j in range(SENT):
        at = lax.rem(chosen[j], H_ROWS)
        value = row_of(halves[j, 0].astype(jnp.float32), at)
        value = value + row_of(wholes[j], lax.rem(chosen[j], F_ROWS))
        if j >= PICKS:
            again = (chosen[j] == chosen[0]) | (chosen[j] == chosen[1])
            value = jnp.where(again, jnp.float32(0.0), value)
            value = row_of(halves[j, 1].astype(jnp.float32), at) + value
        sent.append(value)
    block = jnp.concatenate(sent, axis=0)
    for peer in range(rows.shape[0]):
        rows[peer] = block


def sent_rows(picks, grads, error, copies):
    return pl.pallas_call(
        send_kernel,
        out_shape=jax.ShapeDtypeStruct((copies, SENT, BLOCK), jnp.float32),
        in_specs=[
            pl.BlockSpec(memory_space=pltpu.SMEM),
            pl.BlockSpec(memory_space=pltpu.HBM),
            pl.BlockSpec(memory_space=pltpu.HBM),
        ],
        out_specs=pl.BlockSpec(memory_space=pltpu.VMEM),
        scratch_shapes=[
            pltpu.VMEM((SENT, STEPS, H_ROWS, BLOCK), jnp.bfloat16),
            pltpu.VMEM((SENT, F_ROWS, BLOCK), jnp.float32),
            pltpu.SemaphoreType.DMA((SENT,)),
            pltpu.SemaphoreType.DMA((SENT,)),
        ],
        compiler_params=kernel_params(NEARLY_ALL),
        name="sent_rows",
    )(picks, grads, error)


def error_kernel(picks, table, grads, error, out, hot):
    replica = lax.axis_index("rep")
    size = out.shape[1]
    first = pl.program_id(0) * size
    index = lax.broadcasted_iota(jnp.int32, (size, BLOCK), 0) + first
    value = error[0]
    for step in range(STEPS):
        value = grads[step, 0].astype(jnp.float32) + value
        for k in range(PICKS):
            value = jnp.where(index == picks[step, k, replica], jnp.float32(0.0), value)
    out[0] = value
    order = jnp.concatenate(
        [table[j // PICKS, pl.ds(j % PICKS, 1), :] for j in range(SENT)], axis=1
    )
    index = lax.broadcasted_iota(jnp.int32, hot.shape, 0) + first
    hits = jnp.where(index == order, jnp.float32(1.0), jnp.float32(0.0))
    hot[...] = hits.astype(jnp.bfloat16)


def next_error(picks, grads, error, tiles=4):
    blocks = error.shape[1]
    size = blocks // tiles
    count = SENT * picks.shape[2]
    return pl.pallas_call(
        error_kernel,
        grid=(tiles,),
        out_shape=(
            jax.ShapeDtypeStruct(error.shape, jnp.float32),
            jax.ShapeDtypeStruct((blocks, count), jnp.bfloat16),
        ),
        in_specs=[
            pl.BlockSpec(memory_space=pltpu.SMEM),
            pl.BlockSpec(picks.shape, lambda i: (0, 0, 0)),
            pl.BlockSpec((STEPS, 1, size, BLOCK), lambda i: (0, 0, i, 0)),
            pl.BlockSpec((1, size, BLOCK), lambda i: (0, i, 0)),
        ],
        out_specs=(
            pl.BlockSpec((1, size, BLOCK), lambda i: (0, i, 0)),
            pl.BlockSpec((size, count), lambda i: (i, 0)),
        ),
        compiler_params=kernel_params(),
        cost_estimate=pl.CostEstimate(
            flops=8 * error.size, bytes_accessed=16 * error.size, transcendentals=0
        ),
        name="next_error",
    )(picks, picks, grads, error)


def add_kernel(members, hot, rows, accum, out, turned, sums, sems):
    count = len(members)
    for place, replica in enumerate(members):
        turned[pl.ds(replica, SENT, count), :] = rows[pl.ds(place * SENT, SENT), :]
    value = turned[...]
    high = value.astype(jnp.bfloat16)
    rest = value - high.astype(jnp.float32)
    middle = rest.astype(jnp.bfloat16)
    low = (rest - middle.astype(jnp.float32)).astype(jnp.bfloat16)
    pair = jnp.concatenate([high, middle], axis=1)
    tiles = sems.shape[0]
    size = accum.shape[0] // tiles
    copies = []
    for tile in range(tiles):
        part = pl.ds(tile * size, size)
        both = jnp.dot(hot[part, :], pair, preferred_element_type=jnp.float32)
        small = jnp.dot(hot[part, :], low, preferred_element_type=jnp.float32)
        total = both[:, :BLOCK] + (both[:, BLOCK:] + small)
        sums[part, :] = accum[part, :] + total
        copy = pltpu.make_async_copy(sums.at[part, :], out.at[part, :], sems.at[tile])
        copy.start()
        copies.append(copy)
    for copy in copies:
        copy.wait()


def add_rows(members, hot, rows, accum, tiles=7):
    return pl.pallas_call(
        functools.partial(add_kernel, members),
        out_shape=jax.ShapeDtypeStruct(accum.shape, jnp.float32),
        in_specs=[pl.BlockSpec(memory_space=pltpu.VMEM)] * 3,
        out_specs=pl.BlockSpec(memory_space=pltpu.HBM),
        scratch_shapes=[
            pltpu.VMEM(rows.shape, jnp.float32),
            pltpu.VMEM(accum.shape, jnp.float32),
            pltpu.SemaphoreType.DMA((tiles,)),
        ],
        compiler_params=kernel_params(),
        name="add_rows",
    )(hot, rows, accum)


def exchange_order(count):
    deep = count // WIDE
    first = FIRST_Z * WIDE + FIRST_X
    members = [first]
    for step in range(deep):
        z = (step // 2 + 1) % deep if step % 2 else (deep - step // 2) % deep
        z = (z + EARLY_Z) % deep
        members += [z * WIDE + x for x in range(WIDE) if z * WIDE + x != first]
    return members


def local(grads, error_in, accum_in, picks):
    table = jnp.swapaxes(picks[:, :, 0, :], 1, 2)
    count = lax.axis_size("rep")
    members = exchange_order(count)
    rows = sent_rows(table, grads, error_in, count)
    rows = lax.all_to_all(
        rows, "rep", 0, 0, axis_index_groups=[members], tiled=True
    )
    error, hot = next_error(table, grads, error_in)
    rows = rows.reshape(count * SENT, BLOCK)
    return (add_rows(members, hot, rows, accum_in), error)


def solution(mesh):
    placed = (
        P(None, "rep", "tp", None),
        P("rep", "tp", None),
        P("tp", None),
        P(None, None, "tp", None),
    )
    return jax.shard_map(
        local,
        mesh=mesh,
        in_specs=placed,
        out_specs=(P("tp", None), P("rep", "tp", None)),
        check_vma=False,
    )
```

```python
import functools

import jax
import jax.numpy as jnp
from jax import lax
from jax.experimental import pallas as pl
from jax.experimental.pallas import tpu as pltpu
from jax.sharding import PartitionSpec as P

STEPS = 2
PICKS = 2
BLOCK = 128
SENT = STEPS * PICKS
WIDE = 4
FIRST_Z = 11
FIRST_X = 1
F_ROWS = 8
H_ROWS = 16
KIB = 1024
ROOM = 12 * 1024 * KIB
NEARLY_ALL = (63 * 1024 + 256) * KIB


def kernel_params(limit=ROOM):
    return pltpu.CompilerParams(vmem_limit_bytes=limit)


def send_kernel(picks, grads, error, rows, halves, wholes, half_sems, whole_sems):
    replica = lax.axis_index("rep")
    chosen = [picks[j // PICKS, j % PICKS, replica] for j in range(SENT)]
    copies = []
    for j in range(SENT):
        base = pl.multiple_of((chosen[j] // F_ROWS) * F_ROWS, F_ROWS)
        copies.append(
            pltpu.make_async_copy(
                error.at[0, pl.ds(base, F_ROWS), :], wholes.at[j], whole_sems.at[j]
            )
        )
        base = pl.multiple_of((chosen[j] // H_ROWS) * H_ROWS, H_ROWS)
        steps = pl.ds(0, j // PICKS + 1)
        copies.append(
            pltpu.make_async_copy(
                grads.at[steps, 0, pl.ds(base, H_ROWS), :],
                halves.at[j, steps],
                half_sems.at[j],
            )
        )
    for copy in copies:
        copy.start()
    for copy in copies:
        copy.wait()

    def row_of(tile, at):
        index = lax.broadcasted_iota(jnp.int32, tile.shape, 0)
        kept = jnp.where(index == at, tile, jnp.float32(0.0))
        return jnp.sum(kept, axis=0, keepdims=True)

    sent = []
    for j in range(SENT):
        at = lax.rem(chosen[j], H_ROWS)
        value = row_of(halves[j, 0].astype(jnp.float32), at)
        value = value + row_of(wholes[j], lax.rem(chosen[j], F_ROWS))
        if j >= PICKS:
            again = (chosen[j] == chosen[0]) | (chosen[j] == chosen[1])
            value = jnp.where(again, jnp.float32(0.0), value)
            value = row_of(halves[j, 1].astype(jnp.float32), at) + value
        sent.append(value)
    block = jnp.concatenate(sent, axis=0)
    for peer in range(rows.shape[0]):
        rows[peer] = block


def sent_rows(picks, grads, error, copies):
    return pl.pallas_call(
        send_kernel,
        out_shape=jax.ShapeDtypeStruct((copies, SENT, BLOCK), jnp.float32),
        in_specs=[
            pl.BlockSpec(memory_space=pltpu.SMEM),
            pl.BlockSpec(memory_space=pltpu.HBM),
            pl.BlockSpec(memory_space=pltpu.HBM),
        ],
        out_specs=pl.BlockSpec(memory_space=pltpu.VMEM),
        scratch_shapes=[
            pltpu.VMEM((SENT, STEPS, H_ROWS, BLOCK), jnp.bfloat16),
            pltpu.VMEM((SENT, F_ROWS, BLOCK), jnp.float32),
            pltpu.SemaphoreType.DMA((SENT,)),
            pltpu.SemaphoreType.DMA((SENT,)),
        ],
        compiler_params=kernel_params(NEARLY_ALL),
        name="sent_rows",
    )(picks, grads, error)


def error_kernel(picks, table, grads, error, out, hot):
    replica = lax.axis_index("rep")
    size = out.shape[1]
    first = pl.program_id(0) * size
    index = lax.broadcasted_iota(jnp.int32, (size, BLOCK), 0) + first
    value = error[0]
    for step in range(STEPS):
        value = grads[step, 0].astype(jnp.float32) + value
        for k in range(PICKS):
            value = jnp.where(index == picks[step, k, replica], jnp.float32(0.0), value)
    out[0] = value
    order = jnp.concatenate(
        [table[j // PICKS, pl.ds(j % PICKS, 1), :] for j in range(SENT)], axis=1
    )
    index = lax.broadcasted_iota(jnp.int32, hot.shape, 0) + first
    hits = jnp.where(index == order, jnp.float32(1.0), jnp.float32(0.0))
    hot[...] = hits.astype(jnp.bfloat16)


def next_error(picks, grads, error, tiles=4):
    blocks = error.shape[1]
    size = blocks // tiles
    count = SENT * picks.shape[2]
    return pl.pallas_call(
        error_kernel,
        grid=(tiles,),
        out_shape=(
            jax.ShapeDtypeStruct(error.shape, jnp.float32),
            jax.ShapeDtypeStruct((blocks, count), jnp.bfloat16),
        ),
        in_specs=[
            pl.BlockSpec(memory_space=pltpu.SMEM),
            pl.BlockSpec(picks.shape, lambda i: (0, 0, 0)),
            pl.BlockSpec((STEPS, 1, size, BLOCK), lambda i: (0, 0, i, 0)),
            pl.BlockSpec((1, size, BLOCK), lambda i: (0, i, 0)),
        ],
        out_specs=(
            pl.BlockSpec((1, size, BLOCK), lambda i: (0, i, 0)),
            pl.BlockSpec((size, count), lambda i: (i, 0)),
        ),
        compiler_params=kernel_params(),
        cost_estimate=pl.CostEstimate(
            flops=8 * error.size, bytes_accessed=16 * error.size, transcendentals=0
        ),
        name="next_error",
    )(picks, picks, grads, error)


def add_kernel(members, hot, rows, accum, out, turned, sums, sems):
    count = len(members)
    for place, replica in enumerate(members):
        turned[pl.ds(replica, SENT, count), :] = rows[pl.ds(place * SENT, SENT), :]
    value = turned[...]
    high = value.astype(jnp.bfloat16)
    low = (value - high.astype(jnp.float32)).astype(jnp.bfloat16)
    pair = jnp.concatenate([high, low], axis=1)
    tiles = sems.shape[0]
    size = accum.shape[0] // tiles
    copies = []
    for tile in range(tiles):
        part = pl.ds(tile * size, size)
        both = jnp.dot(hot[part, :], pair, preferred_element_type=jnp.float32)
        sums[part, :] = accum[part, :] + (both[:, :BLOCK] + both[:, BLOCK:])
        copy = pltpu.make_async_copy(sums.at[part, :], out.at[part, :], sems.at[tile])
        copy.start()
        copies.append(copy)
    for copy in copies:
        copy.wait()


def add_rows(members, hot, rows, accum, tiles=7):
    return pl.pallas_call(
        functools.partial(add_kernel, members),
        out_shape=jax.ShapeDtypeStruct(accum.shape, jnp.float32),
        in_specs=[pl.BlockSpec(memory_space=pltpu.VMEM)] * 3,
        out_specs=pl.BlockSpec(memory_space=pltpu.HBM),
        scratch_shapes=[
            pltpu.VMEM(rows.shape, jnp.float32),
            pltpu.VMEM(accum.shape, jnp.float32),
            pltpu.SemaphoreType.DMA((tiles,)),
        ],
        compiler_params=kernel_params(),
        name="add_rows",
    )(hot, rows, accum)


def exchange_order(count):
    first = FIRST_Z * WIDE + FIRST_X
    return [(first + place) % count for place in range(count)]


def local(grads, error_in, accum_in, picks):
    table = jnp.swapaxes(picks[:, :, 0, :], 1, 2)
    count = lax.axis_size("rep")
    members = exchange_order(count)
    rows = sent_rows(table, grads, error_in, count)
    rows = lax.all_to_all(
        rows, "rep", 0, 0, axis_index_groups=[members], tiled=True
    )
    error, hot = next_error(table, grads, error_in)
    rows = rows.reshape(count * SENT, BLOCK)
    return (add_rows(members, hot, rows, accum_in), error)


def solution(mesh):
    placed = (
        P(None, "rep", "tp", None),
        P("rep", "tp", None),
        P("tp", None),
        P(None, None, "tp", None),
    )
    return jax.shard_map(
        local,
        mesh=mesh,
        in_specs=placed,
        out_specs=(P("tp", None), P("rep", "tp", None)),
        check_vma=False,
    )
```

```python
import functools

import jax
import jax.numpy as jnp
from jax import lax
from jax.experimental import pallas as pl
from jax.experimental.pallas import tpu as pltpu
from jax.sharding import PartitionSpec as P

STEPS = 2
PICKS = 2
BLOCK = 128
SENT = STEPS * PICKS
WIDE = 4
FIRST_Z = 11
FIRST_X = 1
F_ROWS = 8
H_ROWS = 16
KIB = 1024
ROOM = 12 * 1024 * KIB


def kernel_params(limit=ROOM):
    return pltpu.CompilerParams(vmem_limit_bytes=limit)


def in_hbm(array):
    return pltpu.with_memory_space_constraint(array, pltpu.HBM)


def send_kernel(picks, grads, error, rows, halves, wholes, half_sems, whole_sems):
    replica = lax.axis_index("rep")
    chosen = [picks[j // PICKS, j % PICKS, replica] for j in range(SENT)]
    copies = []
    for j in range(SENT):
        base = pl.multiple_of((chosen[j] // F_ROWS) * F_ROWS, F_ROWS)
        copies.append(
            pltpu.make_async_copy(
                error.at[0, pl.ds(base, F_ROWS), :], wholes.at[j], whole_sems.at[j]
            )
        )
        base = pl.multiple_of((chosen[j] // H_ROWS) * H_ROWS, H_ROWS)
        steps = pl.ds(0, j // PICKS + 1)
        copies.append(
            pltpu.make_async_copy(
                grads.at[steps, 0, pl.ds(base, H_ROWS), :],
                halves.at[j, steps],
                half_sems.at[j],
            )
        )
    for copy in copies:
        copy.start()
    for copy in copies:
        copy.wait()

    def row_of(tile, at):
        index = lax.broadcasted_iota(jnp.int32, tile.shape, 0)
        kept = jnp.where(index == at, tile, jnp.float32(0.0))
        return jnp.sum(kept, axis=0, keepdims=True)

    sent = []
    for j in range(SENT):
        at = lax.rem(chosen[j], H_ROWS)
        value = row_of(halves[j, 0].astype(jnp.float32), at)
        value = value + row_of(wholes[j], lax.rem(chosen[j], F_ROWS))
        if j >= PICKS:
            again = (chosen[j] == chosen[0]) | (chosen[j] == chosen[1])
            value = jnp.where(again, jnp.float32(0.0), value)
            value = row_of(halves[j, 1].astype(jnp.float32), at) + value
        sent.append(value)
    block = jnp.concatenate(sent, axis=0)
    for peer in range(rows.shape[0]):
        rows[peer] = block


def sent_rows(picks, grads, error, copies):
    return pl.pallas_call(
        send_kernel,
        out_shape=pltpu.VMEM((copies, SENT, BLOCK), jnp.float32),
        in_specs=[
            pl.BlockSpec(memory_space=pltpu.SMEM),
            pl.BlockSpec(memory_space=pltpu.HBM),
            pl.BlockSpec(memory_space=pltpu.HBM),
        ],
        out_specs=pl.BlockSpec(memory_space=pltpu.VMEM),
        scratch_shapes=[
            pltpu.VMEM((SENT, STEPS, H_ROWS, BLOCK), jnp.bfloat16),
            pltpu.VMEM((SENT, F_ROWS, BLOCK), jnp.float32),
            pltpu.SemaphoreType.DMA((SENT,)),
            pltpu.SemaphoreType.DMA((SENT,)),
        ],
        compiler_params=kernel_params(),
        name="sent_rows",
    )(picks, grads, error)


def error_kernel(picks, table, grads, error, out, hot):
    replica = lax.axis_index("rep")
    size = out.shape[1]
    first = pl.program_id(0) * size
    index = lax.broadcasted_iota(jnp.int32, (size, BLOCK), 0) + first
    value = error[0]
    for step in range(STEPS):
        value = grads[step, 0].astype(jnp.float32) + value
        for k in range(PICKS):
            value = jnp.where(index == picks[step, k, replica], jnp.float32(0.0), value)
    out[0] = value
    order = jnp.concatenate(
        [table[j // PICKS, pl.ds(j % PICKS, 1), :] for j in range(SENT)], axis=1
    )
    index = lax.broadcasted_iota(jnp.int32, hot.shape, 0) + first
    hits = jnp.where(index == order, jnp.float32(1.0), jnp.float32(0.0))
    hot[...] = hits.astype(jnp.bfloat16)


def next_error(picks, grads, error, tiles=4):
    blocks = error.shape[1]
    size = blocks // tiles
    count = SENT * picks.shape[2]
    return pl.pallas_call(
        error_kernel,
        grid=(tiles,),
        out_shape=(
            jax.ShapeDtypeStruct(error.shape, jnp.float32),
            jax.ShapeDtypeStruct((blocks, count), jnp.bfloat16),
        ),
        in_specs=[
            pl.BlockSpec(memory_space=pltpu.SMEM),
            pl.BlockSpec(picks.shape, lambda i: (0, 0, 0)),
            pl.BlockSpec((STEPS, 1, size, BLOCK), lambda i: (0, 0, i, 0)),
            pl.BlockSpec((1, size, BLOCK), lambda i: (0, i, 0)),
        ],
        out_specs=(
            pl.BlockSpec((1, size, BLOCK), lambda i: (0, i, 0)),
            pl.BlockSpec((size, count), lambda i: (i, 0)),
        ),
        compiler_params=kernel_params(),
        cost_estimate=pl.CostEstimate(
            flops=8 * error.size, bytes_accessed=16 * error.size, transcendentals=0
        ),
        name="next_error",
    )(picks, picks, grads, error)


def add_kernel(members, hot, rows, accum, out, turned, sums, sems):
    count = len(members)
    for place, replica in enumerate(members):
        turned[pl.ds(replica, SENT, count), :] = rows[pl.ds(place * SENT, SENT), :]
    value = turned[...]
    high = value.astype(jnp.bfloat16)
    low = (value - high.astype(jnp.float32)).astype(jnp.bfloat16)
    pair = jnp.concatenate([high, low], axis=1)
    tiles = sems.shape[0]
    size = accum.shape[0] // tiles
    copies = []
    for tile in range(tiles):
        part = pl.ds(tile * size, size)
        both = jnp.dot(hot[part, :], pair, preferred_element_type=jnp.float32)
        sums[part, :] = accum[part, :] + (both[:, :BLOCK] + both[:, BLOCK:])
        copy = pltpu.make_async_copy(sums.at[part, :], out.at[part, :], sems.at[tile])
        copy.start()
        copies.append(copy)
    for copy in copies:
        copy.wait()


def add_rows(members, hot, rows, accum, tiles=7):
    return pl.pallas_call(
        functools.partial(add_kernel, members),
        out_shape=jax.ShapeDtypeStruct(accum.shape, jnp.float32),
        in_specs=[pl.BlockSpec(memory_space=pltpu.VMEM)] * 3,
        out_specs=pl.BlockSpec(memory_space=pltpu.HBM),
        scratch_shapes=[
            pltpu.VMEM(rows.shape, jnp.float32),
            pltpu.VMEM(accum.shape, jnp.float32),
            pltpu.SemaphoreType.DMA((tiles,)),
        ],
        compiler_params=kernel_params(),
        name="add_rows",
    )(hot, rows, accum)


def exchange_order(count):
    first = FIRST_Z * WIDE + FIRST_X
    return [(first + place) % count for place in range(count)]


def local(grads, error_in, accum_in, picks):
    table = in_hbm(jnp.swapaxes(picks[:, :, 0, :], 1, 2))
    grads, error_in = in_hbm(grads), in_hbm(error_in)
    count = lax.axis_size("rep")
    members = exchange_order(count)
    rows = sent_rows(table, grads, error_in, count)
    rows = lax.all_to_all(
        rows, "rep", 0, 0, axis_index_groups=[members], tiled=True
    )
    error, hot = next_error(table, grads, error_in)
    rows = rows.reshape(count * SENT, BLOCK)
    return (add_rows(members, hot, rows, accum_in), error)


def solution(mesh):
    placed = (
        P(None, "rep", "tp", None),
        P("rep", "tp", None),
        P("tp", None),
        P(None, None, "tp", None),
    )
    return jax.shard_map(
        local,
        mesh=mesh,
        in_specs=placed,
        out_specs=(P("tp", None), P("rep", "tp", None)),
        check_vma=False,
    )
```

```python
import functools

import jax
import jax.numpy as jnp
from jax import lax
from jax.experimental import pallas as pl
from jax.experimental.pallas import tpu as pltpu
from jax.sharding import PartitionSpec as P

STEPS = 2
PICKS = 2
BLOCK = 128
SENT = STEPS * PICKS
WIDE = 4
FIRST_Z = 11
FIRST_X = 1
EARLY_Z = 5
F_ROWS = 8
H_ROWS = 16
KIB = 1024
ROOM = 16 * 1024 * KIB


def kernel_params(limit=ROOM):
    return pltpu.CompilerParams(vmem_limit_bytes=limit)


def in_hbm(array):
    return pltpu.with_memory_space_constraint(array, pltpu.HBM)


def starts_early(replica):
    return replica < EARLY_Z * WIDE


def tile_error(step_tiles, tile_in, own, first):
    index = lax.broadcasted_iota(jnp.int32, tile_in.shape, 0) + first
    left = tile_in
    for step in range(STEPS):
        left = step_tiles[step].astype(jnp.float32) + left
        for k in range(PICKS):
            sent = index == own[step * PICKS + k]
            left = jnp.where(sent, jnp.float32(0.0), left)
    return left


def one_hot(order, first, size):
    index = lax.broadcasted_iota(jnp.int32, (size, order.shape[1]), 0) + first
    hits = jnp.where(index == order, jnp.float32(1.0), jnp.float32(0.0))
    return hits.astype(jnp.bfloat16)


def row_of(tile, at):
    index = lax.broadcasted_iota(jnp.int32, tile.shape, 0)
    kept = jnp.where(index == at, tile, jnp.float32(0.0))
    return jnp.sum(kept, axis=0, keepdims=True)


def prepare_kernel(
    picks, table, grads, error, accum,
    rows, order, own, hot, held, error_out,
    halves, wholes, steps, errors, half_sems, whole_sems, held_sem, sems,
):
    replica = lax.axis_index("rep")
    chosen = [picks[j // PICKS, j % PICKS, replica] for j in range(SENT)]
    copies = []
    for j in range(SENT):
        base = pl.multiple_of((chosen[j] // F_ROWS) * F_ROWS, F_ROWS)
        copies.append(
            pltpu.make_async_copy(
                error.at[0, pl.ds(base, F_ROWS), :], wholes.at[j], whole_sems.at[j]
            )
        )
        base = pl.multiple_of((chosen[j] // H_ROWS) * H_ROWS, H_ROWS)
        part = pl.ds(0, j // PICKS + 1)
        copies.append(
            pltpu.make_async_copy(
                grads.at[part, 0, pl.ds(base, H_ROWS), :],
                halves.at[j, part],
                half_sems.at[j],
            )
        )
    for copy in copies:
        copy.start()
    order[...] = jnp.concatenate(
        [table[j // PICKS, pl.ds(j % PICKS, 1), :] for j in range(SENT)], axis=1
    )
    for j in range(SENT):
        own[pl.ds(j, 1), :] = jnp.full((1, BLOCK), chosen[j], jnp.int32)
    for copy in copies:
        copy.wait()

    sent = []
    for j in range(SENT):
        at = lax.rem(chosen[j], H_ROWS)
        value = row_of(halves[j, 0].astype(jnp.float32), at)
        value = value + row_of(wholes[j], lax.rem(chosen[j], F_ROWS))
        if j >= PICKS:
            again = (chosen[j] == chosen[0]) | (chosen[j] == chosen[1])
            value = jnp.where(again, jnp.float32(0.0), value)
            value = row_of(halves[j, 1].astype(jnp.float32), at) + value
        sent.append(value)
    block = jnp.concatenate(sent, axis=0)
    for peer in range(rows.shape[0]):
        rows[peer] = block

    tiles = sems.shape[1]
    size = errors.shape[0] // tiles

    @pl.when(starts_early(replica))
    def _():
        hold = pltpu.make_async_copy(accum, held, held_sem)
        loads, stores = [], []
        for tile in range(tiles):
            part = pl.ds(tile * size, size)
            loads.append((
                pltpu.make_async_copy(
                    grads.at[:, 0, part, :], steps.at[:, part, :], sems.at[0, tile]
                ),
                pltpu.make_async_copy(
                    error.at[0, part, :], errors.at[part, :], sems.at[1, tile]
                ),
            ))
            for load in loads[-1]:
                load.start()
        hold.start()
        for tile in range(tiles):
            part = pl.ds(tile * size, size)
            hot[part, :] = one_hot(order[...], tile * size, size)
            for load in loads[tile]:
                load.wait()
            pair = [steps[step, part, :] for step in range(STEPS)]
            errors[part, :] = tile_error(pair, errors[part, :], chosen, tile * size)
            stores.append(
                pltpu.make_async_copy(
                    errors.at[part, :], error_out.at[0, part, :], sems.at[2, tile]
                )
            )
            stores[-1].start()
        hold.wait()
        for store in stores:
            store.wait()


def prepare(picks, grads, error, accum, tiles=7):
    blocks = accum.shape[0]
    count = picks.shape[2]
    return pl.pallas_call(
        prepare_kernel,
        out_shape=(
            pltpu.VMEM((count, SENT, BLOCK), jnp.float32),
            pltpu.VMEM((1, SENT * count), jnp.int32),
            pltpu.VMEM((F_ROWS, BLOCK), jnp.int32),
            pltpu.VMEM((blocks, SENT * count), jnp.bfloat16),
            pltpu.VMEM(accum.shape, jnp.float32),
            pltpu.HBM(error.shape, jnp.float32),
        ),
        in_specs=[
            pl.BlockSpec(memory_space=pltpu.SMEM),
            pl.BlockSpec(memory_space=pltpu.VMEM),
        ]
        + [pl.BlockSpec(memory_space=pltpu.HBM)] * 3,
        out_specs=tuple(
            [pl.BlockSpec(memory_space=pltpu.VMEM)] * 5
            + [pl.BlockSpec(memory_space=pltpu.HBM)]
        ),
        scratch_shapes=[
            pltpu.VMEM((SENT, STEPS, H_ROWS, BLOCK), jnp.bfloat16),
            pltpu.VMEM((SENT, F_ROWS, BLOCK), jnp.float32),
            pltpu.VMEM((STEPS,) + accum.shape, jnp.bfloat16),
            pltpu.VMEM(accum.shape, jnp.float32),
            pltpu.SemaphoreType.DMA((SENT,)),
            pltpu.SemaphoreType.DMA((SENT,)),
            pltpu.SemaphoreType.DMA(()),
            pltpu.SemaphoreType.DMA((3, tiles)),
        ],
        compiler_params=kernel_params(),
        name="prepare",
    )(picks, picks, grads, error, accum)


def finish_kernel(
    members, order, own, hot, held, rows, grads, error, accum, _,
    error_out, accum_out, turned, steps, errors, sums, sems,
):
    replica = lax.axis_index("rep")
    tiles = sems.shape[1]
    size = sums.shape[0] // tiles
    count = len(members)
    for place, owner in enumerate(members):
        turned[pl.ds(owner, SENT, count), :] = rows[pl.ds(place * SENT, SENT), :]
    value = turned[...]
    high = value.astype(jnp.bfloat16)
    low = (value - high.astype(jnp.float32)).astype(jnp.bfloat16)
    pair = jnp.concatenate([high, low], axis=1)

    def store_sum(tile, hot_tile, base):
        part = pl.ds(tile * size, size)
        both = jnp.dot(hot_tile, pair, preferred_element_type=jnp.float32)
        sums[part, :] = base + (both[:, :BLOCK] + both[:, BLOCK:])
        copy = pltpu.make_async_copy(
            sums.at[part, :], accum_out.at[part, :], sems.at[0, tile]
        )
        copy.start()
        return copy

    early = starts_early(replica)

    @pl.when(early)
    def _():
        stores = []
        for tile in range(tiles):
            part = pl.ds(tile * size, size)
            stores.append(store_sum(tile, hot[part, :], held[part, :]))
        for store in stores:
            store.wait()

    @pl.when(jnp.logical_not(early))
    def _():
        loads, stores = [], []
        for tile in range(tiles):
            part = pl.ds(tile * size, size)
            loads.append((
                pltpu.make_async_copy(
                    accum.at[part, :], sums.at[part, :], sems.at[1, tile]
                ),
                pltpu.make_async_copy(
                    grads.at[:, 0, part, :], steps.at[:, part, :], sems.at[2, tile]
                ),
                pltpu.make_async_copy(
                    error.at[0, part, :], errors.at[part, :], sems.at[3, tile]
                ),
            ))
            for load in loads[-1]:
                load.start()
        mine = [own[pl.ds(j, 1), :] for j in range(SENT)]
        for tile in range(tiles):
            part = pl.ds(tile * size, size)
            hot_tile = one_hot(order[...], tile * size, size)
            for load in loads[tile]:
                load.wait()
            stores.append(store_sum(tile, hot_tile, sums[part, :]))
            step_tiles = [steps[step, part, :] for step in range(STEPS)]
            errors[part, :] = tile_error(step_tiles, errors[part, :], mine, tile * size)
            stores.append(
                pltpu.make_async_copy(
                    errors.at[part, :], error_out.at[0, part, :], sems.at[4, tile]
                )
            )
            stores[-1].start()
        for store in stores:
            store.wait()


def finish(members, order, own, hot, held, rows, grads, error, accum, done, tiles=7):
    return pl.pallas_call(
        functools.partial(finish_kernel, members),
        out_shape=(
            pltpu.HBM(error.shape, jnp.float32),
            pltpu.HBM(accum.shape, jnp.float32),
        ),
        in_specs=[pl.BlockSpec(memory_space=pltpu.VMEM)] * 5
        + [pl.BlockSpec(memory_space=pltpu.HBM)] * 4,
        out_specs=(
            pl.BlockSpec(memory_space=pltpu.HBM),
            pl.BlockSpec(memory_space=pltpu.HBM),
        ),
        input_output_aliases={8: 0},
        scratch_shapes=[
            pltpu.VMEM(rows.shape, jnp.float32),
            pltpu.VMEM((STEPS,) + accum.shape, jnp.bfloat16),
            pltpu.VMEM(accum.shape, jnp.float32),
            pltpu.VMEM(accum.shape, jnp.float32),
            pltpu.SemaphoreType.DMA((5, tiles)),
        ],
        compiler_params=kernel_params(),
        name="finish",
    )(order, own, hot, held, rows, grads, error, accum, done)


def exchange_order(count):
    first = FIRST_Z * WIDE + FIRST_X
    return [(first + place) % count for place in range(count)]


def local(grads, error_in, accum_in, picks):
    table = in_hbm(jnp.swapaxes(picks[:, :, 0, :], 1, 2))
    grads, error_in, accum_in = in_hbm(grads), in_hbm(error_in), in_hbm(accum_in)
    count = lax.axis_size("rep")
    members = exchange_order(count)
    rows, order, own, hot, held, done = prepare(table, grads, error_in, accum_in)
    rows = lax.all_to_all(
        rows, "rep", 0, 0, axis_index_groups=[members], tiled=True
    )
    rows = rows.reshape(count * SENT, BLOCK)
    error, accum = finish(
        members, order, own, hot, held, rows, grads, error_in, accum_in, in_hbm(done)
    )
    return (accum, error)


def solution(mesh):
    placed = (
        P(None, "rep", "tp", None),
        P("rep", "tp", None),
        P("tp", None),
        P(None, None, "tp", None),
    )
    return jax.shard_map(
        local,
        mesh=mesh,
        in_specs=placed,
        out_specs=(P("tp", None), P("rep", "tp", None)),
        check_vma=False,
    )
```

```python
import functools

import jax
import jax.numpy as jnp
from jax import lax
from jax.experimental import pallas as pl
from jax.experimental.pallas import tpu as pltpu
from jax.sharding import PartitionSpec as P

STEPS = 2
PICKS = 2
BLOCK = 128
SENT = STEPS * PICKS
WIDE = 4
FIRST_Z = 11
FIRST_X = 1
EARLY_Z = 5
F_ROWS = 8
H_ROWS = 16
KIB = 1024
ROOM = 16 * 1024 * KIB


def kernel_params(limit=ROOM):
    return pltpu.CompilerParams(vmem_limit_bytes=limit)


def in_hbm(array):
    return pltpu.with_memory_space_constraint(array, pltpu.HBM)


def starts_early(replica):
    return replica < EARLY_Z * WIDE


def tile_error(step_tiles, tile_in, own, first):
    index = lax.broadcasted_iota(jnp.int32, tile_in.shape, 0) + first
    left = tile_in
    for step in range(STEPS):
        left = step_tiles[step].astype(jnp.float32) + left
        for k in range(PICKS):
            sent = index == own[step * PICKS + k]
            left = jnp.where(sent, jnp.float32(0.0), left)
    return left


def one_hot(order, first, size):
    index = lax.broadcasted_iota(jnp.int32, (size, order.shape[1]), 0) + first
    hits = jnp.where(index == order, jnp.float32(1.0), jnp.float32(0.0))
    return hits.astype(jnp.bfloat16)


def row_of(tile, at):
    index = lax.broadcasted_iota(jnp.int32, tile.shape, 0)
    kept = jnp.where(index == at, tile, jnp.float32(0.0))
    return jnp.sum(kept, axis=0, keepdims=True)


def prepare_kernel(
    picks, table, grads, error, accum,
    rows, order, own, hot, held, error_out,
    lanes, halves, wholes, steps, errors, half_sems, whole_sems, one_sems, sems,
):
    replica = lax.axis_index("rep")
    look = pltpu.make_async_copy(table, lanes, one_sems.at[0])
    look.start()
    chosen = [picks[j // PICKS, j % PICKS, replica] for j in range(SENT)]
    copies = []
    for j in range(SENT):
        base = pl.multiple_of((chosen[j] // F_ROWS) * F_ROWS, F_ROWS)
        copies.append(
            pltpu.make_async_copy(
                error.at[0, pl.ds(base, F_ROWS), :], wholes.at[j], whole_sems.at[j]
            )
        )
        base = pl.multiple_of((chosen[j] // H_ROWS) * H_ROWS, H_ROWS)
        part = pl.ds(0, j // PICKS + 1)
        copies.append(
            pltpu.make_async_copy(
                grads.at[part, 0, pl.ds(base, H_ROWS), :],
                halves.at[j, part],
                half_sems.at[j],
            )
        )
    for copy in copies:
        copy.start()
    look.wait()
    order[...] = jnp.concatenate(
        [lanes[j // PICKS, pl.ds(j % PICKS, 1), :] for j in range(SENT)], axis=1
    )
    for j in range(SENT):
        own[pl.ds(j, 1), :] = jnp.full((1, BLOCK), chosen[j], jnp.int32)
    for copy in copies:
        copy.wait()

    sent = []
    for j in range(SENT):
        at = lax.rem(chosen[j], H_ROWS)
        value = row_of(halves[j, 0].astype(jnp.float32), at)
        value = value + row_of(wholes[j], lax.rem(chosen[j], F_ROWS))
        if j >= PICKS:
            again = (chosen[j] == chosen[0]) | (chosen[j] == chosen[1])
            value = jnp.where(again, jnp.float32(0.0), value)
            value = row_of(halves[j, 1].astype(jnp.float32), at) + value
        sent.append(value)
    block = jnp.concatenate(sent, axis=0)
    for peer in range(rows.shape[0]):
        rows[peer] = block

    tiles = sems.shape[1]
    size = errors.shape[0] // tiles

    @pl.when(starts_early(replica))
    def _():
        hold = pltpu.make_async_copy(accum, held, one_sems.at[1])
        loads, stores = [], []
        for tile in range(tiles):
            part = pl.ds(tile * size, size)
            loads.append((
                pltpu.make_async_copy(
                    grads.at[:, 0, part, :], steps.at[:, part, :], sems.at[0, tile]
                ),
                pltpu.make_async_copy(
                    error.at[0, part, :], errors.at[part, :], sems.at[1, tile]
                ),
            ))
            for load in loads[-1]:
                load.start()
        hold.start()
        for tile in range(tiles):
            part = pl.ds(tile * size, size)
            hot[part, :] = one_hot(order[...], tile * size, size)
            for load in loads[tile]:
                load.wait()
            pair = [steps[step, part, :] for step in range(STEPS)]
            errors[part, :] = tile_error(pair, errors[part, :], chosen, tile * size)
            stores.append(
                pltpu.make_async_copy(
                    errors.at[part, :], error_out.at[0, part, :], sems.at[2, tile]
                )
            )
            stores[-1].start()
        hold.wait()
        for store in stores:
            store.wait()


def prepare(picks, grads, error, accum, tiles=7):
    blocks = accum.shape[0]
    count = picks.shape[2]
    return pl.pallas_call(
        prepare_kernel,
        out_shape=(
            pltpu.VMEM((count, SENT, BLOCK), jnp.float32),
            pltpu.VMEM((1, SENT * count), jnp.int32),
            pltpu.VMEM((F_ROWS, BLOCK), jnp.int32),
            pltpu.VMEM((blocks, SENT * count), jnp.bfloat16),
            pltpu.VMEM(accum.shape, jnp.float32),
            pltpu.HBM(error.shape, jnp.float32),
        ),
        in_specs=[pl.BlockSpec(memory_space=pltpu.SMEM)]
        + [pl.BlockSpec(memory_space=pltpu.HBM)] * 4,
        out_specs=tuple(
            [pl.BlockSpec(memory_space=pltpu.VMEM)] * 5
            + [pl.BlockSpec(memory_space=pltpu.HBM)]
        ),
        scratch_shapes=[
            pltpu.VMEM(picks.shape, jnp.int32),
            pltpu.VMEM((SENT, STEPS, H_ROWS, BLOCK), jnp.bfloat16),
            pltpu.VMEM((SENT, F_ROWS, BLOCK), jnp.float32),
            pltpu.VMEM((STEPS,) + accum.shape, jnp.bfloat16),
            pltpu.VMEM(accum.shape, jnp.float32),
            pltpu.SemaphoreType.DMA((SENT,)),
            pltpu.SemaphoreType.DMA((SENT,)),
            pltpu.SemaphoreType.DMA((2,)),
            pltpu.SemaphoreType.DMA((3, tiles)),
        ],
        compiler_params=kernel_params(),
        name="prepare",
    )(picks, picks, grads, error, accum)


def finish_kernel(
    members, order, own, hot, held, rows, grads, error, accum, _,
    error_out, accum_out, turned, steps, errors, sums, sems,
):
    replica = lax.axis_index("rep")
    tiles = sems.shape[1]
    size = sums.shape[0] // tiles
    count = len(members)

    def split_rows():
        for place, owner in enumerate(members):
            turned[pl.ds(owner, SENT, count), :] = rows[pl.ds(place * SENT, SENT), :]
        value = turned[...]
        high = value.astype(jnp.bfloat16)
        low = (value - high.astype(jnp.float32)).astype(jnp.bfloat16)
        return jnp.concatenate([high, low], axis=1)

    def store_sum(tile, hot_tile, pair, base):
        part = pl.ds(tile * size, size)
        both = jnp.dot(hot_tile, pair, preferred_element_type=jnp.float32)
        sums[part, :] = base + (both[:, :BLOCK] + both[:, BLOCK:])
        copy = pltpu.make_async_copy(
            sums.at[part, :], accum_out.at[part, :], sems.at[0, tile]
        )
        copy.start()
        return copy

    early = starts_early(replica)

    @pl.when(early)
    def _():
        pair = split_rows()
        stores = []
        for tile in range(tiles):
            part = pl.ds(tile * size, size)
            stores.append(store_sum(tile, hot[part, :], pair, held[part, :]))
        for store in stores:
            store.wait()

    @pl.when(jnp.logical_not(early))
    def _():
        loads, stores = [], []
        for tile in range(tiles):
            part = pl.ds(tile * size, size)
            loads.append((
                pltpu.make_async_copy(
                    accum.at[part, :], sums.at[part, :], sems.at[1, tile]
                ),
                pltpu.make_async_copy(
                    grads.at[:, 0, part, :], steps.at[:, part, :], sems.at[2, tile]
                ),
                pltpu.make_async_copy(
                    error.at[0, part, :], errors.at[part, :], sems.at[3, tile]
                ),
            ))
            for load in loads[-1]:
                load.start()
        pair = split_rows()
        mine = [own[pl.ds(j, 1), :] for j in range(SENT)]
        for tile in range(tiles):
            part = pl.ds(tile * size, size)
            hot_tile = one_hot(order[...], tile * size, size)
            for load in loads[tile]:
                load.wait()
            stores.append(store_sum(tile, hot_tile, pair, sums[part, :]))
            step_tiles = [steps[step, part, :] for step in range(STEPS)]
            errors[part, :] = tile_error(step_tiles, errors[part, :], mine, tile * size)
            stores.append(
                pltpu.make_async_copy(
                    errors.at[part, :], error_out.at[0, part, :], sems.at[4, tile]
                )
            )
            stores[-1].start()
        for store in stores:
            store.wait()


def finish(members, order, own, hot, held, rows, grads, error, accum, done, tiles=7):
    return pl.pallas_call(
        functools.partial(finish_kernel, members),
        out_shape=(
            pltpu.HBM(error.shape, jnp.float32),
            pltpu.HBM(accum.shape, jnp.float32),
        ),
        in_specs=[pl.BlockSpec(memory_space=pltpu.VMEM)] * 5
        + [pl.BlockSpec(memory_space=pltpu.HBM)] * 4,
        out_specs=(
            pl.BlockSpec(memory_space=pltpu.HBM),
            pl.BlockSpec(memory_space=pltpu.HBM),
        ),
        input_output_aliases={8: 0},
        scratch_shapes=[
            pltpu.VMEM(rows.shape, jnp.float32),
            pltpu.VMEM((STEPS,) + accum.shape, jnp.bfloat16),
            pltpu.VMEM(accum.shape, jnp.float32),
            pltpu.VMEM(accum.shape, jnp.float32),
            pltpu.SemaphoreType.DMA((5, tiles)),
        ],
        compiler_params=kernel_params(),
        name="finish",
    )(order, own, hot, held, rows, grads, error, accum, done)


def exchange_order(count):
    first = FIRST_Z * WIDE + FIRST_X
    return [(first + place) % count for place in range(count)]


def local(grads, error_in, accum_in, picks):
    table = in_hbm(jnp.swapaxes(picks[:, :, 0, :], 1, 2))
    grads, error_in, accum_in = in_hbm(grads), in_hbm(error_in), in_hbm(accum_in)
    count = lax.axis_size("rep")
    members = exchange_order(count)
    rows, order, own, hot, held, done = prepare(table, grads, error_in, accum_in)
    rows = lax.all_to_all(
        rows, "rep", 0, 0, axis_index_groups=[members], tiled=True
    )
    rows = rows.reshape(count * SENT, BLOCK)
    error, accum = finish(
        members, order, own, hot, held, rows, grads, error_in, accum_in, in_hbm(done)
    )
    return (accum, error)


def solution(mesh):
    placed = (
        P(None, "rep", "tp", None),
        P("rep", "tp", None),
        P("tp", None),
        P(None, None, "tp", None),
    )
    return jax.shard_map(
        local,
        mesh=mesh,
        in_specs=placed,
        out_specs=(P("tp", None), P("rep", "tp", None)),
        check_vma=False,
    )
```

```python
import functools

import jax
import jax.numpy as jnp
from jax import lax
from jax.experimental import pallas as pl
from jax.experimental.pallas import tpu as pltpu
from jax.sharding import PartitionSpec as P

STEPS = 2
PICKS = 2
BLOCK = 128
SENT = STEPS * PICKS
WIDE = 4
FIRST_Z = 11
FIRST_X = 1
EARLY_Z = 5
F_ROWS = 8
H_ROWS = 16
KIB = 1024
ROOM = 16 * 1024 * KIB


def kernel_params(limit=ROOM):
    return pltpu.CompilerParams(vmem_limit_bytes=limit)


def in_hbm(array):
    return pltpu.with_memory_space_constraint(array, pltpu.HBM)


def starts_early(replica):
    return replica < EARLY_Z * WIDE


def tile_error(step_tiles, tile_in, own, first):
    index = lax.broadcasted_iota(jnp.int32, tile_in.shape, 0) + first
    left = tile_in
    for step in range(STEPS):
        left = step_tiles[step].astype(jnp.float32) + left
        for k in range(PICKS):
            sent = index == own[step * PICKS + k]
            left = jnp.where(sent, jnp.float32(0.0), left)
    return left


def one_hot(order, first, size):
    index = lax.broadcasted_iota(jnp.int32, (size, order.shape[1]), 0) + first
    hits = jnp.where(index == order, jnp.float32(1.0), jnp.float32(0.0))
    return hits.astype(jnp.bfloat16)


def row_of(tile, at):
    index = lax.broadcasted_iota(jnp.int32, tile.shape, 0)
    kept = jnp.where(index == at, tile, jnp.float32(0.0))
    return jnp.sum(kept, axis=0, keepdims=True)


def prepare_kernel(
    picks, grads, error, accum,
    rows, order, own, hot, held, error_out,
    spots, lanes, steps, errors, one_sems, load_sems, store_sems,
):
    replica = lax.axis_index("rep")
    look = pltpu.make_async_copy(picks, spots, one_sems.at[0])
    look.start()
    loads = []
    chunks = load_sems.shape[1]
    size = errors.shape[0] // chunks
    for chunk in range(chunks):
        part = pl.ds(chunk * size, size)
        loads.append(
            pltpu.make_async_copy(
                error.at[0, part, :], errors.at[part, :], load_sems.at[0, chunk]
            )
        )
        loads.append(
            pltpu.make_async_copy(
                grads.at[:, 0, part, :], steps.at[:, part, :], load_sems.at[1, chunk]
            )
        )
    for load in loads:
        load.start()
    scan = pltpu.make_async_copy(picks, lanes, one_sems.at[1])
    scan.start()
    look.wait()
    chosen = [spots[j // PICKS, j % PICKS, replica] for j in range(SENT)]
    for j in range(SENT):
        own[pl.ds(j, 1), :] = jnp.full((1, BLOCK), chosen[j], jnp.int32)
    scan.wait()
    order[...] = jnp.concatenate(
        [lanes[j // PICKS, pl.ds(j % PICKS, 1), :] for j in range(SENT)], axis=1
    )
    for load in loads:
        load.wait()

    sent = []
    for j in range(SENT):
        base = pl.multiple_of((chosen[j] // H_ROWS) * H_ROWS, H_ROWS)
        at = chosen[j] - base
        near = pl.ds(base, H_ROWS)
        value = steps[0, near, :].astype(jnp.float32) + errors[near, :]
        if j >= PICKS:
            again = (chosen[j] == chosen[0]) | (chosen[j] == chosen[1])
            value = jnp.where(again, jnp.float32(0.0), value)
            value = steps[1, near, :].astype(jnp.float32) + value
        sent.append(row_of(value, at))
    block = jnp.concatenate(sent, axis=0)
    for peer in range(rows.shape[0]):
        rows[peer] = block

    @pl.when(starts_early(replica))
    def _():
        hold = pltpu.make_async_copy(accum, held, one_sems.at[2])
        hold.start()
        tiles = store_sems.shape[0]
        size = errors.shape[0] // tiles
        stores = []
        for tile in range(tiles):
            part = pl.ds(tile * size, size)
            hot[part, :] = one_hot(order[...], tile * size, size)
            pair = [steps[step, part, :] for step in range(STEPS)]
            errors[part, :] = tile_error(pair, errors[part, :], chosen, tile * size)
            stores.append(
                pltpu.make_async_copy(
                    errors.at[part, :], error_out.at[0, part, :], store_sems.at[tile]
                )
            )
            stores[-1].start()
        hold.wait()
        for store in stores:
            store.wait()


def prepare(picks, grads, error, accum, chunks=4, tiles=7):
    blocks = accum.shape[0]
    count = picks.shape[2]
    return pl.pallas_call(
        prepare_kernel,
        out_shape=(
            pltpu.VMEM((count, SENT, BLOCK), jnp.float32),
            pltpu.VMEM((1, SENT * count), jnp.int32),
            pltpu.VMEM((F_ROWS, BLOCK), jnp.int32),
            pltpu.VMEM((blocks, SENT * count), jnp.bfloat16),
            pltpu.VMEM(accum.shape, jnp.float32),
            pltpu.HBM(error.shape, jnp.float32),
        ),
        in_specs=[pl.BlockSpec(memory_space=pltpu.HBM)] * 4,
        out_specs=tuple(
            [pl.BlockSpec(memory_space=pltpu.VMEM)] * 5
            + [pl.BlockSpec(memory_space=pltpu.HBM)]
        ),
        scratch_shapes=[
            pltpu.SMEM(picks.shape, jnp.int32),
            pltpu.VMEM(picks.shape, jnp.int32),
            pltpu.VMEM((STEPS,) + accum.shape, jnp.bfloat16),
            pltpu.VMEM(accum.shape, jnp.float32),
            pltpu.SemaphoreType.DMA((3,)),
            pltpu.SemaphoreType.DMA((2, chunks)),
            pltpu.SemaphoreType.DMA((tiles,)),
        ],
        compiler_params=kernel_params(),
        name="prepare",
    )(picks, grads, error, accum)


def finish_kernel(
    members, order, own, hot, held, rows, grads, error, accum, _,
    error_out, accum_out, turned, steps, errors, sums, sems,
):
    replica = lax.axis_index("rep")
    tiles = sems.shape[1]
    size = sums.shape[0] // tiles
    count = len(members)

    def split_rows():
        for place, owner in enumerate(members):
            turned[pl.ds(owner, SENT, count), :] = rows[pl.ds(place * SENT, SENT), :]
        value = turned[...]
        high = value.astype(jnp.bfloat16)
        low = (value - high.astype(jnp.float32)).astype(jnp.bfloat16)
        return jnp.concatenate([high, low], axis=1)

    def store_sum(tile, hot_tile, pair, base):
        part = pl.ds(tile * size, size)
        both = jnp.dot(hot_tile, pair, preferred_element_type=jnp.float32)
        sums[part, :] = base + (both[:, :BLOCK] + both[:, BLOCK:])
        copy = pltpu.make_async_copy(
            sums.at[part, :], accum_out.at[part, :], sems.at[0, tile]
        )
        copy.start()
        return copy

    early = starts_early(replica)

    @pl.when(early)
    def _():
        pair = split_rows()
        stores = []
        for tile in range(tiles):
            part = pl.ds(tile * size, size)
            stores.append(store_sum(tile, hot[part, :], pair, held[part, :]))
        for store in stores:
            store.wait()

    @pl.when(jnp.logical_not(early))
    def _():
        loads, stores = [], []
        for tile in range(tiles):
            part = pl.ds(tile * size, size)
            loads.append((
                pltpu.make_async_copy(
                    accum.at[part, :], sums.at[part, :], sems.at[1, tile]
                ),
                pltpu.make_async_copy(
                    grads.at[:, 0, part, :], steps.at[:, part, :], sems.at[2, tile]
                ),
                pltpu.make_async_copy(
                    error.at[0, part, :], errors.at[part, :], sems.at[3, tile]
                ),
            ))
            for load in loads[-1]:
                load.start()
        pair = split_rows()
        mine = [own[pl.ds(j, 1), :] for j in range(SENT)]
        for tile in range(tiles):
            part = pl.ds(tile * size, size)
            hot_tile = one_hot(order[...], tile * size, size)
            for load in loads[tile]:
                load.wait()
            stores.append(store_sum(tile, hot_tile, pair, sums[part, :]))
            step_tiles = [steps[step, part, :] for step in range(STEPS)]
            errors[part, :] = tile_error(step_tiles, errors[part, :], mine, tile * size)
            stores.append(
                pltpu.make_async_copy(
                    errors.at[part, :], error_out.at[0, part, :], sems.at[4, tile]
                )
            )
            stores[-1].start()
        for store in stores:
            store.wait()


def finish(members, order, own, hot, held, rows, grads, error, accum, done, tiles=7):
    return pl.pallas_call(
        functools.partial(finish_kernel, members),
        out_shape=(
            pltpu.HBM(error.shape, jnp.float32),
            pltpu.HBM(accum.shape, jnp.float32),
        ),
        in_specs=[pl.BlockSpec(memory_space=pltpu.VMEM)] * 5
        + [pl.BlockSpec(memory_space=pltpu.HBM)] * 4,
        out_specs=(
            pl.BlockSpec(memory_space=pltpu.HBM),
            pl.BlockSpec(memory_space=pltpu.HBM),
        ),
        input_output_aliases={8: 0},
        scratch_shapes=[
            pltpu.VMEM(rows.shape, jnp.float32),
            pltpu.VMEM((STEPS,) + accum.shape, jnp.bfloat16),
            pltpu.VMEM(accum.shape, jnp.float32),
            pltpu.VMEM(accum.shape, jnp.float32),
            pltpu.SemaphoreType.DMA((5, tiles)),
        ],
        compiler_params=kernel_params(),
        name="finish",
    )(order, own, hot, held, rows, grads, error, accum, done)


def exchange_order(count):
    first = FIRST_Z * WIDE + FIRST_X
    return [(first + place) % count for place in range(count)]


def local(grads, error_in, accum_in, picks):
    table = in_hbm(jnp.swapaxes(picks[:, :, 0, :], 1, 2))
    grads, error_in, accum_in = in_hbm(grads), in_hbm(error_in), in_hbm(accum_in)
    count = lax.axis_size("rep")
    members = exchange_order(count)
    rows, order, own, hot, held, done = prepare(table, grads, error_in, accum_in)
    rows = lax.all_to_all(
        rows, "rep", 0, 0, axis_index_groups=[members], tiled=True
    )
    rows = rows.reshape(count * SENT, BLOCK)
    error, accum = finish(
        members, order, own, hot, held, rows, grads, error_in, accum_in, in_hbm(done)
    )
    return (accum, error)


def solution(mesh):
    placed = (
        P(None, "rep", "tp", None),
        P("rep", "tp", None),
        P("tp", None),
        P(None, None, "tp", None),
    )
    return jax.shard_map(
        local,
        mesh=mesh,
        in_specs=placed,
        out_specs=(P("tp", None), P("rep", "tp", None)),
        check_vma=False,
    )
```

```python
import functools

import jax
import jax.numpy as jnp
from jax import lax
from jax.experimental import pallas as pl
from jax.experimental.pallas import tpu as pltpu
from jax.sharding import PartitionSpec as P

STEPS = 2
PICKS = 2
BLOCK = 128
SENT = STEPS * PICKS
WIDE = 4
FIRST_Z = 10
FIRST_X = 2
EARLY_Z = 5
EARLY_TILES = (256, 512, 512, 256, 128, 128)
F_ROWS = 8
H_ROWS = 16
KIB = 1024
ROOM = 16 * 1024 * KIB


def kernel_params(limit=ROOM):
    return pltpu.CompilerParams(vmem_limit_bytes=limit)


def in_hbm(array):
    return pltpu.with_memory_space_constraint(array, pltpu.HBM)


def starts_early(replica):
    return replica < EARLY_Z * WIDE


def tile_error(step_tiles, tile_in, own, first):
    index = lax.broadcasted_iota(jnp.int32, tile_in.shape, 0) + first
    left = tile_in
    for step in range(STEPS):
        left = step_tiles[step].astype(jnp.float32) + left
        for k in range(PICKS):
            sent = index == own[step * PICKS + k]
            left = jnp.where(sent, jnp.float32(0.0), left)
    return left


def one_hot(order, first, size):
    index = lax.broadcasted_iota(jnp.int32, (size, order.shape[1]), 0) + first
    hits = jnp.where(index == order, jnp.float32(1.0), jnp.float32(0.0))
    return hits.astype(jnp.bfloat16)


def row_of(tile, at):
    index = lax.broadcasted_iota(jnp.int32, tile.shape, 0)
    kept = jnp.where(index == at, tile, jnp.float32(0.0))
    return jnp.sum(kept, axis=0, keepdims=True)


def prepare_kernel(
    picks, grads, error, accum,
    rows, order, own, hot, held, error_out,
    spots, lanes, steps, errors, one_sems, load_sems, store_sems,
):
    replica = lax.axis_index("rep")
    look = pltpu.make_async_copy(picks, spots, one_sems.at[0])
    look.start()
    loads = []
    chunks = load_sems.shape[1]
    size = errors.shape[0] // chunks
    for chunk in range(chunks):
        part = pl.ds(chunk * size, size)
        loads.append(
            pltpu.make_async_copy(
                error.at[0, part, :], errors.at[part, :], load_sems.at[0, chunk]
            )
        )
        loads.append(
            pltpu.make_async_copy(
                grads.at[:, 0, part, :], steps.at[:, part, :], load_sems.at[1, chunk]
            )
        )
    for load in loads:
        load.start()
    scan = pltpu.make_async_copy(picks, lanes, one_sems.at[1])
    scan.start()
    look.wait()
    chosen = [spots[j // PICKS, j % PICKS, replica] for j in range(SENT)]
    for j in range(SENT):
        own[pl.ds(j, 1), :] = jnp.full((1, BLOCK), chosen[j], jnp.int32)
    scan.wait()
    order[...] = jnp.concatenate(
        [lanes[j // PICKS, pl.ds(j % PICKS, 1), :] for j in range(SENT)], axis=1
    )
    for load in loads:
        load.wait()

    sent = []
    for j in range(SENT):
        base = pl.multiple_of((chosen[j] // H_ROWS) * H_ROWS, H_ROWS)
        at = chosen[j] - base
        near = pl.ds(base, H_ROWS)
        value = steps[0, near, :].astype(jnp.float32) + errors[near, :]
        if j >= PICKS:
            again = (chosen[j] == chosen[0]) | (chosen[j] == chosen[1])
            value = jnp.where(again, jnp.float32(0.0), value)
            value = steps[1, near, :].astype(jnp.float32) + value
        sent.append(row_of(value, at))
    block = jnp.concatenate(sent, axis=0)
    for peer in range(rows.shape[0]):
        rows[peer] = block

    @pl.when(starts_early(replica))
    def _():
        hold = pltpu.make_async_copy(accum, held, one_sems.at[2])
        hold.start()
        tiles = store_sems.shape[0]
        size = errors.shape[0] // tiles
        stores = []
        for tile in range(tiles):
            part = pl.ds(tile * size, size)
            hot[part, :] = one_hot(order[...], tile * size, size)
            pair = [steps[step, part, :] for step in range(STEPS)]
            errors[part, :] = tile_error(pair, errors[part, :], chosen, tile * size)
            stores.append(
                pltpu.make_async_copy(
                    errors.at[part, :], error_out.at[0, part, :], store_sems.at[tile]
                )
            )
            stores[-1].start()
        hold.wait()
        for store in stores:
            store.wait()


def prepare(picks, grads, error, accum, chunks=4, tiles=7):
    blocks = accum.shape[0]
    count = picks.shape[2]
    return pl.pallas_call(
        prepare_kernel,
        out_shape=(
            pltpu.VMEM((count, SENT, BLOCK), jnp.float32),
            pltpu.VMEM((1, SENT * count), jnp.int32),
            pltpu.VMEM((F_ROWS, BLOCK), jnp.int32),
            pltpu.VMEM((blocks, SENT * count), jnp.bfloat16),
            pltpu.VMEM(accum.shape, jnp.float32),
            pltpu.HBM(error.shape, jnp.float32),
        ),
        in_specs=[pl.BlockSpec(memory_space=pltpu.HBM)] * 4,
        out_specs=tuple(
            [pl.BlockSpec(memory_space=pltpu.VMEM)] * 5
            + [pl.BlockSpec(memory_space=pltpu.HBM)]
        ),
        scratch_shapes=[
            pltpu.SMEM(picks.shape, jnp.int32),
            pltpu.VMEM(picks.shape, jnp.int32),
            pltpu.VMEM((STEPS,) + accum.shape, jnp.bfloat16),
            pltpu.VMEM(accum.shape, jnp.float32),
            pltpu.SemaphoreType.DMA((3,)),
            pltpu.SemaphoreType.DMA((2, chunks)),
            pltpu.SemaphoreType.DMA((tiles,)),
        ],
        compiler_params=kernel_params(),
        name="prepare",
    )(picks, grads, error, accum)


def finish_kernel(
    members, order, own, hot, held, rows, grads, error, accum, _,
    error_out, accum_out, turned, steps, errors, sums, sems,
):
    replica = lax.axis_index("rep")
    tiles = sems.shape[1]
    size = sums.shape[0] // tiles
    count = len(members)

    def split_rows():
        for place, owner in enumerate(members):
            turned[pl.ds(owner, SENT, count), :] = rows[pl.ds(place * SENT, SENT), :]
        value = turned[...]
        high = value.astype(jnp.bfloat16)
        low = (value - high.astype(jnp.float32)).astype(jnp.bfloat16)
        return jnp.concatenate([high, low], axis=1)

    def store_sum(tile, part, hot_tile, pair, base):
        both = jnp.dot(hot_tile, pair, preferred_element_type=jnp.float32)
        sums[part, :] = base + (both[:, :BLOCK] + both[:, BLOCK:])
        copy = pltpu.make_async_copy(
            sums.at[part, :], accum_out.at[part, :], sems.at[0, tile]
        )
        copy.start()
        return copy

    early = starts_early(replica)

    @pl.when(early)
    def _():
        pair = split_rows()
        stores = []
        first = 0
        for tile, size in enumerate(EARLY_TILES):
            part = pl.ds(first, size)
            first += size
            stores.append(store_sum(tile, part, hot[part, :], pair, held[part, :]))
        for store in stores:
            store.wait()

    @pl.when(jnp.logical_not(early))
    def _():
        loads, stores = [], []
        for tile in range(tiles):
            part = pl.ds(tile * size, size)
            loads.append((
                pltpu.make_async_copy(
                    accum.at[part, :], sums.at[part, :], sems.at[1, tile]
                ),
                pltpu.make_async_copy(
                    grads.at[:, 0, part, :], steps.at[:, part, :], sems.at[2, tile]
                ),
                pltpu.make_async_copy(
                    error.at[0, part, :], errors.at[part, :], sems.at[3, tile]
                ),
            ))
            for load in loads[-1]:
                load.start()
        pair = split_rows()
        mine = [own[pl.ds(j, 1), :] for j in range(SENT)]
        for tile in range(tiles):
            part = pl.ds(tile * size, size)
            hot_tile = one_hot(order[...], tile * size, size)
            for load in loads[tile]:
                load.wait()
            stores.append(store_sum(tile, part, hot_tile, pair, sums[part, :]))
            step_tiles = [steps[step, part, :] for step in range(STEPS)]
            errors[part, :] = tile_error(step_tiles, errors[part, :], mine, tile * size)
            stores.append(
                pltpu.make_async_copy(
                    errors.at[part, :], error_out.at[0, part, :], sems.at[4, tile]
                )
            )
            stores[-1].start()
        for store in stores:
            store.wait()


def finish(members, order, own, hot, held, rows, grads, error, accum, done, tiles=7):
    return pl.pallas_call(
        functools.partial(finish_kernel, members),
        out_shape=(
            pltpu.HBM(error.shape, jnp.float32),
            pltpu.HBM(accum.shape, jnp.float32),
        ),
        in_specs=[pl.BlockSpec(memory_space=pltpu.VMEM)] * 5
        + [pl.BlockSpec(memory_space=pltpu.HBM)] * 4,
        out_specs=(
            pl.BlockSpec(memory_space=pltpu.HBM),
            pl.BlockSpec(memory_space=pltpu.HBM),
        ),
        input_output_aliases={8: 0},
        scratch_shapes=[
            pltpu.VMEM(rows.shape, jnp.float32),
            pltpu.VMEM((STEPS,) + accum.shape, jnp.bfloat16),
            pltpu.VMEM(accum.shape, jnp.float32),
            pltpu.VMEM(accum.shape, jnp.float32),
            pltpu.SemaphoreType.DMA((5, tiles)),
        ],
        compiler_params=kernel_params(),
        name="finish",
    )(order, own, hot, held, rows, grads, error, accum, done)


def exchange_order(count):
    first = FIRST_Z * WIDE + FIRST_X
    return [(first + place) % count for place in range(count)]


def local(grads, error_in, accum_in, picks):
    table = in_hbm(jnp.swapaxes(picks[:, :, 0, :], 1, 2))
    grads, error_in, accum_in = in_hbm(grads), in_hbm(error_in), in_hbm(accum_in)
    count = lax.axis_size("rep")
    members = exchange_order(count)
    rows, order, own, hot, held, done = prepare(table, grads, error_in, accum_in)
    rows = lax.all_to_all(
        rows, "rep", 0, 0, axis_index_groups=[members], tiled=True
    )
    rows = rows.reshape(count * SENT, BLOCK)
    error, accum = finish(
        members, order, own, hot, held, rows, grads, error_in, accum_in, in_hbm(done)
    )
    return (accum, error)


def solution(mesh):
    placed = (
        P(None, "rep", "tp", None),
        P("rep", "tp", None),
        P("tp", None),
        P(None, None, "tp", None),
    )
    return jax.shard_map(
        local,
        mesh=mesh,
        in_specs=placed,
        out_specs=(P("tp", None), P("rep", "tp", None)),
        check_vma=False,
    )
```

```python
import functools

import jax
import jax.numpy as jnp
from jax import lax
from jax.experimental import pallas as pl
from jax.experimental.pallas import tpu as pltpu
from jax.sharding import PartitionSpec as P

STEPS = 2
PICKS = 2
BLOCK = 128
SENT = STEPS * PICKS
WIDE = 4
FIRST_Z = 11
FIRST_X = 2
EARLY_Z = 5
EARLY_TILES = (256,) * 7
F_ROWS = 8
H_ROWS = 16
KIB = 1024
ROOM = 16 * 1024 * KIB


def kernel_params(limit=ROOM):
    return pltpu.CompilerParams(vmem_limit_bytes=limit)


def in_hbm(array):
    return pltpu.with_memory_space_constraint(array, pltpu.HBM)


def starts_early(replica):
    return replica < EARLY_Z * WIDE


def tile_error(step_tiles, tile_in, own, first):
    index = lax.broadcasted_iota(jnp.int32, tile_in.shape, 0) + first
    left = tile_in
    for step in range(STEPS):
        left = step_tiles[step].astype(jnp.float32) + left
        for k in range(PICKS):
            sent = index == own[step * PICKS + k]
            left = jnp.where(sent, jnp.float32(0.0), left)
    return left


def one_hot(order, first, size):
    index = lax.broadcasted_iota(jnp.int32, (size, order.shape[1]), 0) + first
    hits = jnp.where(index == order, jnp.float32(1.0), jnp.float32(0.0))
    return hits.astype(jnp.bfloat16)


def row_of(tile, at):
    index = lax.broadcasted_iota(jnp.int32, tile.shape, 0)
    kept = jnp.where(index == at, tile, jnp.float32(0.0))
    return jnp.sum(kept, axis=0, keepdims=True)


def prepare_kernel(
    picks, grads, error, accum,
    rows, order, own, hot, held, error_out,
    spots, lanes, steps, errors, one_sems, load_sems, store_sems,
):
    replica = lax.axis_index("rep")
    look = pltpu.make_async_copy(picks, spots, one_sems.at[0])
    look.start()
    loads = []
    chunks = load_sems.shape[1]
    size = errors.shape[0] // chunks
    for chunk in range(chunks):
        part = pl.ds(chunk * size, size)
        loads.append(
            pltpu.make_async_copy(
                error.at[0, part, :], errors.at[part, :], load_sems.at[0, chunk]
            )
        )
        loads.append(
            pltpu.make_async_copy(
                grads.at[:, 0, part, :], steps.at[:, part, :], load_sems.at[1, chunk]
            )
        )
    for load in loads:
        load.start()
    scan = pltpu.make_async_copy(picks, lanes, one_sems.at[1])
    scan.start()
    look.wait()
    chosen = [spots[j // PICKS, j % PICKS, replica] for j in range(SENT)]
    for j in range(SENT):
        own[pl.ds(j, 1), :] = jnp.full((1, BLOCK), chosen[j], jnp.int32)
    scan.wait()
    order[...] = jnp.concatenate(
        [lanes[j // PICKS, pl.ds(j % PICKS, 1), :] for j in range(SENT)], axis=1
    )
    for load in loads:
        load.wait()

    sent = []
    for j in range(SENT):
        base = pl.multiple_of((chosen[j] // H_ROWS) * H_ROWS, H_ROWS)
        at = chosen[j] - base
        near = pl.ds(base, H_ROWS)
        value = steps[0, near, :].astype(jnp.float32) + errors[near, :]
        if j >= PICKS:
            again = (chosen[j] == chosen[0]) | (chosen[j] == chosen[1])
            value = jnp.where(again, jnp.float32(0.0), value)
            value = steps[1, near, :].astype(jnp.float32) + value
        sent.append(row_of(value, at))
    block = jnp.concatenate(sent, axis=0)
    for peer in range(rows.shape[0]):
        rows[peer] = block

    @pl.when(starts_early(replica))
    def _():
        hold = pltpu.make_async_copy(accum, held, one_sems.at[2])
        hold.start()
        tiles = store_sems.shape[0]
        size = errors.shape[0] // tiles
        stores = []
        for tile in range(tiles):
            part = pl.ds(tile * size, size)
            hot[part, :] = one_hot(order[...], tile * size, size)
            pair = [steps[step, part, :] for step in range(STEPS)]
            errors[part, :] = tile_error(pair, errors[part, :], chosen, tile * size)
            stores.append(
                pltpu.make_async_copy(
                    errors.at[part, :], error_out.at[0, part, :], store_sems.at[tile]
                )
            )
            stores[-1].start()
        hold.wait()
        for store in stores:
            store.wait()


def prepare(picks, grads, error, accum, chunks=4, tiles=7):
    blocks = accum.shape[0]
    count = picks.shape[2]
    return pl.pallas_call(
        prepare_kernel,
        out_shape=(
            pltpu.VMEM((count, SENT, BLOCK), jnp.float32),
            pltpu.VMEM((1, SENT * count), jnp.int32),
            pltpu.VMEM((F_ROWS, BLOCK), jnp.int32),
            pltpu.VMEM((blocks, SENT * count), jnp.bfloat16),
            pltpu.VMEM(accum.shape, jnp.float32),
            pltpu.HBM(error.shape, jnp.float32),
        ),
        in_specs=[pl.BlockSpec(memory_space=pltpu.HBM)] * 4,
        out_specs=tuple(
            [pl.BlockSpec(memory_space=pltpu.VMEM)] * 5
            + [pl.BlockSpec(memory_space=pltpu.HBM)]
        ),
        scratch_shapes=[
            pltpu.SMEM(picks.shape, jnp.int32),
            pltpu.VMEM(picks.shape, jnp.int32),
            pltpu.VMEM((STEPS,) + accum.shape, jnp.bfloat16),
            pltpu.VMEM(accum.shape, jnp.float32),
            pltpu.SemaphoreType.DMA((3,)),
            pltpu.SemaphoreType.DMA((2, chunks)),
            pltpu.SemaphoreType.DMA((tiles,)),
        ],
        compiler_params=kernel_params(),
        name="prepare",
    )(picks, grads, error, accum)


def finish_kernel(
    members, order, own, hot, held, rows, grads, error, accum, _,
    error_out, accum_out, turned, steps, errors, sums, sems,
):
    replica = lax.axis_index("rep")
    tiles = sems.shape[1]
    size = sums.shape[0] // tiles
    count = len(members)

    def split_rows():
        for place, owner in enumerate(members):
            turned[pl.ds(owner, SENT, count), :] = rows[pl.ds(place * SENT, SENT), :]
        value = turned[...]
        high = value.astype(jnp.bfloat16)
        low = (value - high.astype(jnp.float32)).astype(jnp.bfloat16)
        return jnp.concatenate([high, low], axis=1)

    def store_sum(tile, part, hot_tile, pair, base):
        both = jnp.dot(hot_tile, pair, preferred_element_type=jnp.float32)
        sums[part, :] = base + (both[:, :BLOCK] + both[:, BLOCK:])
        copy = pltpu.make_async_copy(
            sums.at[part, :], accum_out.at[part, :], sems.at[0, tile]
        )
        copy.start()
        return copy

    early = starts_early(replica)

    @pl.when(early)
    def _():
        pair = split_rows()
        stores = []
        first = 0
        for tile, size in enumerate(EARLY_TILES):
            part = pl.ds(first, size)
            first += size
            stores.append(store_sum(tile, part, hot[part, :], pair, held[part, :]))
        for store in stores:
            store.wait()

    @pl.when(jnp.logical_not(early))
    def _():
        loads, stores = [], []
        for tile in range(tiles):
            part = pl.ds(tile * size, size)
            loads.append((
                pltpu.make_async_copy(
                    accum.at[part, :], sums.at[part, :], sems.at[1, tile]
                ),
                pltpu.make_async_copy(
                    grads.at[:, 0, part, :], steps.at[:, part, :], sems.at[2, tile]
                ),
                pltpu.make_async_copy(
                    error.at[0, part, :], errors.at[part, :], sems.at[3, tile]
                ),
            ))
            for load in loads[-1]:
                load.start()
        pair = split_rows()
        mine = [own[pl.ds(j, 1), :] for j in range(SENT)]
        for tile in range(tiles):
            part = pl.ds(tile * size, size)
            hot_tile = one_hot(order[...], tile * size, size)
            for load in loads[tile]:
                load.wait()
            stores.append(store_sum(tile, part, hot_tile, pair, sums[part, :]))
            step_tiles = [steps[step, part, :] for step in range(STEPS)]
            errors[part, :] = tile_error(step_tiles, errors[part, :], mine, tile * size)
            stores.append(
                pltpu.make_async_copy(
                    errors.at[part, :], error_out.at[0, part, :], sems.at[4, tile]
                )
            )
            stores[-1].start()
        for store in stores:
            store.wait()


def finish(members, order, own, hot, held, rows, grads, error, accum, done, tiles=7):
    return pl.pallas_call(
        functools.partial(finish_kernel, members),
        out_shape=(
            pltpu.HBM(error.shape, jnp.float32),
            pltpu.HBM(accum.shape, jnp.float32),
        ),
        in_specs=[pl.BlockSpec(memory_space=pltpu.VMEM)] * 5
        + [pl.BlockSpec(memory_space=pltpu.HBM)] * 4,
        out_specs=(
            pl.BlockSpec(memory_space=pltpu.HBM),
            pl.BlockSpec(memory_space=pltpu.HBM),
        ),
        input_output_aliases={8: 0},
        scratch_shapes=[
            pltpu.VMEM(rows.shape, jnp.float32),
            pltpu.VMEM((STEPS,) + accum.shape, jnp.bfloat16),
            pltpu.VMEM(accum.shape, jnp.float32),
            pltpu.VMEM(accum.shape, jnp.float32),
            pltpu.SemaphoreType.DMA((5, tiles)),
        ],
        compiler_params=kernel_params(),
        name="finish",
    )(order, own, hot, held, rows, grads, error, accum, done)


def exchange_order(count):
    first = FIRST_Z * WIDE + FIRST_X
    return [(first + place) % count for place in range(count)]


def local(grads, error_in, accum_in, picks):
    table = in_hbm(jnp.swapaxes(picks[:, :, 0, :], 1, 2))
    grads, error_in, accum_in = in_hbm(grads), in_hbm(error_in), in_hbm(accum_in)
    count = lax.axis_size("rep")
    members = exchange_order(count)
    rows, order, own, hot, held, done = prepare(table, grads, error_in, accum_in)
    rows = lax.all_to_all(
        rows, "rep", 0, 0, axis_index_groups=[members], tiled=True
    )
    rows = rows.reshape(count * SENT, BLOCK)
    error, accum = finish(
        members, order, own, hot, held, rows, grads, error_in, accum_in, in_hbm(done)
    )
    return (accum, error)


def solution(mesh):
    placed = (
        P(None, "rep", "tp", None),
        P("rep", "tp", None),
        P("tp", None),
        P(None, None, "tp", None),
    )
    return jax.shard_map(
        local,
        mesh=mesh,
        in_specs=placed,
        out_specs=(P("tp", None), P("rep", "tp", None)),
        check_vma=False,
    )
```

```python
import functools

import jax
import jax.numpy as jnp
from jax import lax
from jax.experimental import pallas as pl
from jax.experimental.pallas import tpu as pltpu
from jax.sharding import PartitionSpec as P

STEPS = 2
PICKS = 2
BLOCK = 128
SENT = STEPS * PICKS
WIDE = 4
FIRST_Z = 12
FIRST_X = 2
EARLY_Z = 5
EARLY_TILES = (256,) * 7
F_ROWS = 8
H_ROWS = 16
KIB = 1024
ROOM = 16 * 1024 * KIB


def kernel_params(limit=ROOM):
    return pltpu.CompilerParams(vmem_limit_bytes=limit)


def in_hbm(array):
    return pltpu.with_memory_space_constraint(array, pltpu.HBM)


def starts_early(replica):
    return replica < EARLY_Z * WIDE


def tile_error(step_tiles, tile_in, own, first):
    index = lax.broadcasted_iota(jnp.int32, tile_in.shape, 0) + first
    left = tile_in
    for step in range(STEPS):
        left = step_tiles[step].astype(jnp.float32) + left
        for k in range(PICKS):
            sent = index == own[step * PICKS + k]
            left = jnp.where(sent, jnp.float32(0.0), left)
    return left


def one_hot(order, first, size):
    index = lax.broadcasted_iota(jnp.int32, (size, order.shape[1]), 0) + first
    hits = jnp.where(index == order, jnp.float32(1.0), jnp.float32(0.0))
    return hits.astype(jnp.bfloat16)


def row_of(tile, at):
    index = lax.broadcasted_iota(jnp.int32, tile.shape, 0)
    kept = jnp.where(index == at, tile, jnp.float32(0.0))
    return jnp.sum(kept, axis=0, keepdims=True)


def prepare_kernel(
    picks, grads, error, accum,
    rows, order, own, hot, held, error_out,
    spots, lanes, steps, errors, one_sems, load_sems, store_sems,
):
    replica = lax.axis_index("rep")
    look = pltpu.make_async_copy(picks, spots, one_sems.at[0])
    look.start()
    loads = []
    chunks = load_sems.shape[1]
    size = errors.shape[0] // chunks
    for chunk in range(chunks):
        part = pl.ds(chunk * size, size)
        loads.append(
            pltpu.make_async_copy(
                error.at[0, part, :], errors.at[part, :], load_sems.at[0, chunk]
            )
        )
        loads.append(
            pltpu.make_async_copy(
                grads.at[:, 0, part, :], steps.at[:, part, :], load_sems.at[1, chunk]
            )
        )
    for load in loads:
        load.start()
    scan = pltpu.make_async_copy(picks, lanes, one_sems.at[1])
    scan.start()
    look.wait()
    chosen = [spots[j // PICKS, j % PICKS, replica] for j in range(SENT)]
    for j in range(SENT):
        own[pl.ds(j, 1), :] = jnp.full((1, BLOCK), chosen[j], jnp.int32)
    scan.wait()
    order[...] = jnp.concatenate(
        [lanes[j // PICKS, pl.ds(j % PICKS, 1), :] for j in range(SENT)], axis=1
    )
    for load in loads:
        load.wait()

    sent = []
    for j in range(SENT):
        base = pl.multiple_of((chosen[j] // H_ROWS) * H_ROWS, H_ROWS)
        at = chosen[j] - base
        near = pl.ds(base, H_ROWS)
        value = steps[0, near, :].astype(jnp.float32) + errors[near, :]
        if j >= PICKS:
            again = (chosen[j] == chosen[0]) | (chosen[j] == chosen[1])
            value = jnp.where(again, jnp.float32(0.0), value)
            value = steps[1, near, :].astype(jnp.float32) + value
        sent.append(row_of(value, at))
    block = jnp.concatenate(sent, axis=0)
    for peer in range(rows.shape[0]):
        rows[peer] = block

    @pl.when(starts_early(replica))
    def _():
        hold = pltpu.make_async_copy(accum, held, one_sems.at[2])
        hold.start()
        tiles = store_sems.shape[0]
        size = errors.shape[0] // tiles
        stores = []
        for tile in range(tiles):
            part = pl.ds(tile * size, size)
            hot[part, :] = one_hot(order[...], tile * size, size)
            pair = [steps[step, part, :] for step in range(STEPS)]
            errors[part, :] = tile_error(pair, errors[part, :], chosen, tile * size)
            stores.append(
                pltpu.make_async_copy(
                    errors.at[part, :], error_out.at[0, part, :], store_sems.at[tile]
                )
            )
            stores[-1].start()
        hold.wait()
        for store in stores:
            store.wait()


def prepare(picks, grads, error, accum, chunks=4, tiles=7):
    blocks = accum.shape[0]
    count = picks.shape[2]
    return pl.pallas_call(
        prepare_kernel,
        out_shape=(
            pltpu.VMEM((count, SENT, BLOCK), jnp.float32),
            pltpu.VMEM((1, SENT * count), jnp.int32),
            pltpu.VMEM((F_ROWS, BLOCK), jnp.int32),
            pltpu.VMEM((blocks, SENT * count), jnp.bfloat16),
            pltpu.VMEM(accum.shape, jnp.float32),
            pltpu.HBM(error.shape, jnp.float32),
        ),
        in_specs=[pl.BlockSpec(memory_space=pltpu.HBM)] * 4,
        out_specs=tuple(
            [pl.BlockSpec(memory_space=pltpu.VMEM)] * 5
            + [pl.BlockSpec(memory_space=pltpu.HBM)]
        ),
        scratch_shapes=[
            pltpu.SMEM(picks.shape, jnp.int32),
            pltpu.VMEM(picks.shape, jnp.int32),
            pltpu.VMEM((STEPS,) + accum.shape, jnp.bfloat16),
            pltpu.VMEM(accum.shape, jnp.float32),
            pltpu.SemaphoreType.DMA((3,)),
            pltpu.SemaphoreType.DMA((2, chunks)),
            pltpu.SemaphoreType.DMA((tiles,)),
        ],
        compiler_params=kernel_params(),
        name="prepare",
    )(picks, grads, error, accum)


def finish_kernel(
    members, order, own, hot, held, rows, grads, error, accum, _,
    error_out, accum_out, turned, steps, errors, sums, sems,
):
    replica = lax.axis_index("rep")
    tiles = sems.shape[1]
    size = sums.shape[0] // tiles
    count = len(members)

    def split_rows():
        for place, owner in enumerate(members):
            turned[pl.ds(owner, SENT, count), :] = rows[pl.ds(place * SENT, SENT), :]
        value = turned[...]
        high = value.astype(jnp.bfloat16)
        low = (value - high.astype(jnp.float32)).astype(jnp.bfloat16)
        return jnp.concatenate([high, low], axis=1)

    def store_sum(tile, part, hot_tile, pair, base):
        both = jnp.dot(hot_tile, pair, preferred_element_type=jnp.float32)
        sums[part, :] = base + (both[:, :BLOCK] + both[:, BLOCK:])
        copy = pltpu.make_async_copy(
            sums.at[part, :], accum_out.at[part, :], sems.at[0, tile]
        )
        copy.start()
        return copy

    early = starts_early(replica)

    @pl.when(early)
    def _():
        pair = split_rows()
        stores = []
        first = 0
        for tile, size in enumerate(EARLY_TILES):
            part = pl.ds(first, size)
            first += size
            stores.append(store_sum(tile, part, hot[part, :], pair, held[part, :]))
        for store in stores:
            store.wait()

    @pl.when(jnp.logical_not(early))
    def _():
        loads, stores = [], []
        for tile in range(tiles):
            part = pl.ds(tile * size, size)
            loads.append((
                pltpu.make_async_copy(
                    accum.at[part, :], sums.at[part, :], sems.at[1, tile]
                ),
                pltpu.make_async_copy(
                    grads.at[:, 0, part, :], steps.at[:, part, :], sems.at[2, tile]
                ),
                pltpu.make_async_copy(
                    error.at[0, part, :], errors.at[part, :], sems.at[3, tile]
                ),
            ))
            for load in loads[-1]:
                load.start()
        pair = split_rows()
        mine = [own[pl.ds(j, 1), :] for j in range(SENT)]
        for tile in range(tiles):
            part = pl.ds(tile * size, size)
            hot_tile = one_hot(order[...], tile * size, size)
            for load in loads[tile]:
                load.wait()
            stores.append(store_sum(tile, part, hot_tile, pair, sums[part, :]))
            step_tiles = [steps[step, part, :] for step in range(STEPS)]
            errors[part, :] = tile_error(step_tiles, errors[part, :], mine, tile * size)
            stores.append(
                pltpu.make_async_copy(
                    errors.at[part, :], error_out.at[0, part, :], sems.at[4, tile]
                )
            )
            stores[-1].start()
        for store in stores:
            store.wait()


def finish(members, order, own, hot, held, rows, grads, error, accum, done, tiles=7):
    return pl.pallas_call(
        functools.partial(finish_kernel, members),
        out_shape=(
            pltpu.HBM(error.shape, jnp.float32),
            pltpu.HBM(accum.shape, jnp.float32),
        ),
        in_specs=[pl.BlockSpec(memory_space=pltpu.VMEM)] * 5
        + [pl.BlockSpec(memory_space=pltpu.HBM)] * 4,
        out_specs=(
            pl.BlockSpec(memory_space=pltpu.HBM),
            pl.BlockSpec(memory_space=pltpu.HBM),
        ),
        input_output_aliases={8: 0},
        scratch_shapes=[
            pltpu.VMEM(rows.shape, jnp.float32),
            pltpu.VMEM((STEPS,) + accum.shape, jnp.bfloat16),
            pltpu.VMEM(accum.shape, jnp.float32),
            pltpu.VMEM(accum.shape, jnp.float32),
            pltpu.SemaphoreType.DMA((5, tiles)),
        ],
        compiler_params=kernel_params(),
        name="finish",
    )(order, own, hot, held, rows, grads, error, accum, done)


def exchange_order(count):
    first = FIRST_Z * WIDE + FIRST_X
    return [(first + place) % count for place in range(count)]


def local(grads, error_in, accum_in, picks):
    table = in_hbm(jnp.swapaxes(picks[:, :, 0, :], 1, 2))
    grads, error_in, accum_in = in_hbm(grads), in_hbm(error_in), in_hbm(accum_in)
    count = lax.axis_size("rep")
    members = exchange_order(count)
    rows, order, own, hot, held, done = prepare(table, grads, error_in, accum_in)
    rows = lax.all_to_all(
        rows, "rep", 0, 0, axis_index_groups=[members], tiled=True
    )
    rows = rows.reshape(count * SENT, BLOCK)
    error, accum = finish(
        members, order, own, hot, held, rows, grads, error_in, accum_in, in_hbm(done)
    )
    return (accum, error)


def solution(mesh):
    placed = (
        P(None, "rep", "tp", None),
        P("rep", "tp", None),
        P("tp", None),
        P(None, None, "tp", None),
    )
    return jax.shard_map(
        local,
        mesh=mesh,
        in_specs=placed,
        out_specs=(P("tp", None), P("rep", "tp", None)),
        check_vma=False,
    )
```

```python
import jax
import jax.numpy as jnp
from jax import lax
from jax.experimental import pallas as pl
from jax.experimental.pallas import tpu as pltpu
from jax.sharding import PartitionSpec as P

STEPS = 2
PICKS = 2
BLOCK = 128
SENT = STEPS * PICKS
WIDE = 4
FIRST = 11 * WIDE + 2
EARLY_Z = 5
EARLY_TILES = (256,) * 7
F_ROWS = 8
H_ROWS = 16
KIB = 1024
ROOM = 16 * 1024 * KIB


def kernel_params(limit=ROOM):
    return pltpu.CompilerParams(vmem_limit_bytes=limit)


def in_hbm(array):
    return pltpu.with_memory_space_constraint(array, pltpu.HBM)


def starts_early(replica):
    return replica < EARLY_Z * WIDE


def tile_error(step_tiles, tile_in, own, first):
    index = lax.broadcasted_iota(jnp.int32, tile_in.shape, 0) + first
    left = tile_in
    for step in range(STEPS):
        left = step_tiles[step].astype(jnp.float32) + left
        for k in range(PICKS):
            sent = index == own[step * PICKS + k]
            left = jnp.where(sent, jnp.float32(0.0), left)
    return left


def one_hot(order, first, size):
    index = lax.broadcasted_iota(jnp.int32, (size, order.shape[1]), 0) + first
    hits = jnp.where(index == order, jnp.float32(1.0), jnp.float32(0.0))
    return hits.astype(jnp.bfloat16)


def row_of(tile, at):
    index = lax.broadcasted_iota(jnp.int32, tile.shape, 0)
    kept = jnp.where(index == at, tile, jnp.float32(0.0))
    return jnp.sum(kept, axis=0, keepdims=True)


def prepare_kernel(
    picks, grads, error, accum,
    rows, order, own, hot, held, error_out,
    spots, lanes, steps, errors, one_sems, load_sems, store_sems,
):
    replica = lax.axis_index("rep")
    look = pltpu.make_async_copy(picks, spots, one_sems.at[0])
    look.start()
    loads = []
    chunks = load_sems.shape[1]
    size = errors.shape[0] // chunks
    for chunk in range(chunks):
        part = pl.ds(chunk * size, size)
        loads.append(
            pltpu.make_async_copy(
                error.at[0, part, :], errors.at[part, :], load_sems.at[0, chunk]
            )
        )
        loads.append(
            pltpu.make_async_copy(
                grads.at[:, 0, part, :], steps.at[:, part, :], load_sems.at[1, chunk]
            )
        )
    for load in loads:
        load.start()
    scan = pltpu.make_async_copy(picks, lanes, one_sems.at[1])
    scan.start()
    look.wait()
    chosen = [spots[j // PICKS, j % PICKS, replica] for j in range(SENT)]
    for j in range(SENT):
        own[pl.ds(j, 1), :] = jnp.full((1, BLOCK), chosen[j], jnp.int32)
    scan.wait()
    parts = []
    for j in range(SENT):
        lane = lanes[j // PICKS, pl.ds(j % PICKS, 1), :]
        parts += [lane[:, FIRST:], lane[:, :FIRST]]
    order[...] = jnp.concatenate(parts, axis=1)
    for load in loads:
        load.wait()

    sent = []
    for j in range(SENT):
        base = pl.multiple_of((chosen[j] // H_ROWS) * H_ROWS, H_ROWS)
        at = chosen[j] - base
        near = pl.ds(base, H_ROWS)
        value = steps[0, near, :].astype(jnp.float32) + errors[near, :]
        if j >= PICKS:
            again = (chosen[j] == chosen[0]) | (chosen[j] == chosen[1])
            value = jnp.where(again, jnp.float32(0.0), value)
            value = steps[1, near, :].astype(jnp.float32) + value
        sent.append(row_of(value, at))
    block = jnp.concatenate(sent, axis=0)
    for peer in range(rows.shape[0]):
        rows[peer] = block

    @pl.when(starts_early(replica))
    def _():
        hold = pltpu.make_async_copy(accum, held, one_sems.at[2])
        hold.start()
        tiles = store_sems.shape[0]
        size = errors.shape[0] // tiles
        stores = []
        for tile in range(tiles):
            part = pl.ds(tile * size, size)
            hot[part, :] = one_hot(order[...], tile * size, size)
            pair = [steps[step, part, :] for step in range(STEPS)]
            errors[part, :] = tile_error(pair, errors[part, :], chosen, tile * size)
            stores.append(
                pltpu.make_async_copy(
                    errors.at[part, :], error_out.at[0, part, :], store_sems.at[tile]
                )
            )
            stores[-1].start()
        hold.wait()
        for store in stores:
            store.wait()


def prepare(picks, grads, error, accum, chunks=4, tiles=7):
    blocks = accum.shape[0]
    count = picks.shape[2]
    return pl.pallas_call(
        prepare_kernel,
        out_shape=(
            pltpu.VMEM((count, SENT, BLOCK), jnp.float32),
            pltpu.VMEM((1, SENT * count), jnp.int32),
            pltpu.VMEM((F_ROWS, BLOCK), jnp.int32),
            pltpu.VMEM((blocks, SENT * count), jnp.bfloat16),
            pltpu.VMEM(accum.shape, jnp.float32),
            pltpu.HBM(error.shape, jnp.float32),
        ),
        in_specs=[pl.BlockSpec(memory_space=pltpu.HBM)] * 4,
        out_specs=tuple(
            [pl.BlockSpec(memory_space=pltpu.VMEM)] * 5
            + [pl.BlockSpec(memory_space=pltpu.HBM)]
        ),
        scratch_shapes=[
            pltpu.SMEM(picks.shape, jnp.int32),
            pltpu.VMEM(picks.shape, jnp.int32),
            pltpu.VMEM((STEPS,) + accum.shape, jnp.bfloat16),
            pltpu.VMEM(accum.shape, jnp.float32),
            pltpu.SemaphoreType.DMA((3,)),
            pltpu.SemaphoreType.DMA((2, chunks)),
            pltpu.SemaphoreType.DMA((tiles,)),
        ],
        compiler_params=kernel_params(),
        name="prepare",
    )(picks, grads, error, accum)


def finish_kernel(
    order, own, hot, held, rows, grads, error, accum, _,
    error_out, accum_out, steps, errors, sums, sems,
):
    replica = lax.axis_index("rep")
    tiles = sems.shape[1]
    size = sums.shape[0] // tiles
    count = rows.shape[0] // SENT

    def split_rows():
        value = jnp.concatenate(
            [rows[pl.ds(j, count, SENT), :] for j in range(SENT)], axis=0
        )
        high = value.astype(jnp.bfloat16)
        low = (value - high.astype(jnp.float32)).astype(jnp.bfloat16)
        return jnp.concatenate([high, low], axis=1)

    def store_sum(tile, part, hot_tile, pair, base):
        both = jnp.dot(hot_tile, pair, preferred_element_type=jnp.float32)
        sums[part, :] = base + (both[:, :BLOCK] + both[:, BLOCK:])
        copy = pltpu.make_async_copy(
            sums.at[part, :], accum_out.at[part, :], sems.at[0, tile]
        )
        copy.start()
        return copy

    early = starts_early(replica)

    @pl.when(early)
    def _():
        pair = split_rows()
        stores = []
        first = 0
        for tile, size in enumerate(EARLY_TILES):
            part = pl.ds(first, size)
            first += size
            stores.append(store_sum(tile, part, hot[part, :], pair, held[part, :]))
        for store in stores:
            store.wait()

    @pl.when(jnp.logical_not(early))
    def _():
        loads, stores = [], []
        for tile in range(tiles):
            part = pl.ds(tile * size, size)
            loads.append((
                pltpu.make_async_copy(
                    accum.at[part, :], sums.at[part, :], sems.at[1, tile]
                ),
                pltpu.make_async_copy(
                    grads.at[:, 0, part, :], steps.at[:, part, :], sems.at[2, tile]
                ),
                pltpu.make_async_copy(
                    error.at[0, part, :], errors.at[part, :], sems.at[3, tile]
                ),
            ))
            for load in loads[-1]:
                load.start()
        pair = split_rows()
        mine = [own[pl.ds(j, 1), :] for j in range(SENT)]
        for tile in range(tiles):
            part = pl.ds(tile * size, size)
            hot_tile = one_hot(order[...], tile * size, size)
            for load in loads[tile]:
                load.wait()
            stores.append(store_sum(tile, part, hot_tile, pair, sums[part, :]))
            step_tiles = [steps[step, part, :] for step in range(STEPS)]
            errors[part, :] = tile_error(step_tiles, errors[part, :], mine, tile * size)
            stores.append(
                pltpu.make_async_copy(
                    errors.at[part, :], error_out.at[0, part, :], sems.at[4, tile]
                )
            )
            stores[-1].start()
        for store in stores:
            store.wait()


def finish(order, own, hot, held, rows, grads, error, accum, done, tiles=7):
    return pl.pallas_call(
        finish_kernel,
        out_shape=(
            pltpu.HBM(error.shape, jnp.float32),
            pltpu.HBM(accum.shape, jnp.float32),
        ),
        in_specs=[pl.BlockSpec(memory_space=pltpu.VMEM)] * 5
        + [pl.BlockSpec(memory_space=pltpu.HBM)] * 4,
        out_specs=(
            pl.BlockSpec(memory_space=pltpu.HBM),
            pl.BlockSpec(memory_space=pltpu.HBM),
        ),
        input_output_aliases={8: 0},
        scratch_shapes=[
            pltpu.VMEM((STEPS,) + accum.shape, jnp.bfloat16),
            pltpu.VMEM(accum.shape, jnp.float32),
            pltpu.VMEM(accum.shape, jnp.float32),
            pltpu.SemaphoreType.DMA((5, tiles)),
        ],
        compiler_params=kernel_params(),
        name="finish",
    )(order, own, hot, held, rows, grads, error, accum, done)


def exchange_order(count):
    return [(FIRST + place) % count for place in range(count)]


def local(grads, error_in, accum_in, picks):
    table = in_hbm(jnp.swapaxes(picks[:, :, 0, :], 1, 2))
    grads, error_in, accum_in = in_hbm(grads), in_hbm(error_in), in_hbm(accum_in)
    count = lax.axis_size("rep")
    members = exchange_order(count)
    rows, order, own, hot, held, done = prepare(table, grads, error_in, accum_in)
    rows = lax.all_to_all(
        rows, "rep", 0, 0, axis_index_groups=[members], tiled=True
    )
    rows = rows.reshape(count * SENT, BLOCK)
    error, accum = finish(
        order, own, hot, held, rows, grads, error_in, accum_in, in_hbm(done)
    )
    return (accum, error)


def solution(mesh):
    placed = (
        P(None, "rep", "tp", None),
        P("rep", "tp", None),
        P("tp", None),
        P(None, None, "tp", None),
    )
    return jax.shard_map(
        local,
        mesh=mesh,
        in_specs=placed,
        out_specs=(P("tp", None), P("rep", "tp", None)),
        check_vma=False,
    )
```

```python
import jax
import jax.numpy as jnp
from jax import lax
from jax.experimental import pallas as pl
from jax.experimental.pallas import tpu as pltpu
from jax.sharding import PartitionSpec as P

STEPS = 2
PICKS = 2
BLOCK = 128
SENT = STEPS * PICKS
WIDE = 4
FIRST = 11 * WIDE + 2
EARLY_Z = 5
EARLY_TILES = (256,) * 7
F_ROWS = 8
H_ROWS = 16
KIB = 1024
ROOM = 16 * 1024 * KIB


def kernel_params(limit=ROOM):
    return pltpu.CompilerParams(vmem_limit_bytes=limit)


def in_hbm(array):
    return pltpu.with_memory_space_constraint(array, pltpu.HBM)


def starts_early(replica):
    return replica < EARLY_Z * WIDE


def tile_error(step_tiles, tile_in, own, first):
    index = lax.broadcasted_iota(jnp.int32, tile_in.shape, 0) + first
    left = tile_in
    for step in range(STEPS):
        left = step_tiles[step].astype(jnp.float32) + left
        for k in range(PICKS):
            sent = index == own[step * PICKS + k]
            left = jnp.where(sent, jnp.float32(0.0), left)
    return left


def one_hot(order, first, size):
    index = lax.broadcasted_iota(jnp.int32, (size, order.shape[1]), 0) + first
    hits = jnp.where(index == order, jnp.float32(1.0), jnp.float32(0.0))
    return hits.astype(jnp.bfloat16)


def row_of(tile, at):
    index = lax.broadcasted_iota(jnp.int32, tile.shape, 0)
    kept = jnp.where(index == at, tile, jnp.float32(0.0))
    return jnp.sum(kept, axis=0, keepdims=True)


def prepare_kernel(
    picks, grads, error, accum,
    rows, order, own, hot, held, error_out,
    spots, lanes, steps, errors, one_sems, load_sems, store_sems,
):
    replica = lax.axis_index("rep")
    look = pltpu.make_async_copy(picks, spots, one_sems.at[0])
    look.start()
    loads = []
    chunks = load_sems.shape[1]
    size = errors.shape[0] // chunks
    for chunk in range(chunks):
        part = pl.ds(chunk * size, size)
        loads.append(
            pltpu.make_async_copy(
                error.at[0, part, :], errors.at[part, :], load_sems.at[0, chunk]
            )
        )
        loads.append(
            pltpu.make_async_copy(
                grads.at[:, 0, part, :], steps.at[:, part, :], load_sems.at[1, chunk]
            )
        )
    for load in loads:
        load.start()
    scan = pltpu.make_async_copy(picks, lanes, one_sems.at[1])
    scan.start()
    look.wait()
    chosen = [spots[j // PICKS, j % PICKS, replica] for j in range(SENT)]
    for j in range(SENT):
        own[pl.ds(j, 1), :] = jnp.full((1, BLOCK), chosen[j], jnp.int32)
    scan.wait()
    parts = []
    for j in range(SENT):
        lane = lanes[j // PICKS, pl.ds(j % PICKS, 1), :]
        parts += [lane[:, FIRST:], lane[:, :FIRST]]
    order[...] = jnp.concatenate(parts, axis=1)
    for load in loads:
        load.wait()

    sent = []
    for j in range(SENT):
        base = pl.multiple_of((chosen[j] // H_ROWS) * H_ROWS, H_ROWS)
        at = chosen[j] - base
        near = pl.ds(base, H_ROWS)
        value = steps[0, near, :].astype(jnp.float32) + errors[near, :]
        if j >= PICKS:
            again = (chosen[j] == chosen[0]) | (chosen[j] == chosen[1])
            value = jnp.where(again, jnp.float32(0.0), value)
            value = steps[1, near, :].astype(jnp.float32) + value
        sent.append(row_of(value, at))
    block = jnp.concatenate(sent, axis=0)
    for peer in range(rows.shape[0]):
        rows[peer] = block

    @pl.when(starts_early(replica))
    def _():
        hold = pltpu.make_async_copy(accum, held, one_sems.at[2])
        hold.start()
        tiles = store_sems.shape[0]
        size = errors.shape[0] // tiles

        def store(tile):
            part = pl.ds(pl.multiple_of(tile * size, size), size)
            return pltpu.make_async_copy(
                errors.at[part, :], error_out.at[0, part, :], store_sems.at[tile]
            )

        @pl.loop(0, tiles)
        def _(tile):
            part = pl.ds(pl.multiple_of(tile * size, size), size)
            hot[part, :] = one_hot(order[...], tile * size, size)
            pair = [steps[step, part, :] for step in range(STEPS)]
            errors[part, :] = tile_error(pair, errors[part, :], chosen, tile * size)
            store(tile).start()

        hold.wait()

        @pl.loop(0, tiles)
        def _(tile):
            store(tile).wait()


def prepare(picks, grads, error, accum, chunks=4, tiles=7):
    blocks = accum.shape[0]
    count = picks.shape[2]
    return pl.pallas_call(
        prepare_kernel,
        out_shape=(
            pltpu.VMEM((count, SENT, BLOCK), jnp.float32),
            pltpu.VMEM((1, SENT * count), jnp.int32),
            pltpu.VMEM((F_ROWS, BLOCK), jnp.int32),
            pltpu.VMEM((blocks, SENT * count), jnp.bfloat16),
            pltpu.VMEM(accum.shape, jnp.float32),
            pltpu.HBM(error.shape, jnp.float32),
        ),
        in_specs=[pl.BlockSpec(memory_space=pltpu.HBM)] * 4,
        out_specs=tuple(
            [pl.BlockSpec(memory_space=pltpu.VMEM)] * 5
            + [pl.BlockSpec(memory_space=pltpu.HBM)]
        ),
        scratch_shapes=[
            pltpu.SMEM(picks.shape, jnp.int32),
            pltpu.VMEM(picks.shape, jnp.int32),
            pltpu.VMEM((STEPS,) + accum.shape, jnp.bfloat16),
            pltpu.VMEM(accum.shape, jnp.float32),
            pltpu.SemaphoreType.DMA((3,)),
            pltpu.SemaphoreType.DMA((2, chunks)),
            pltpu.SemaphoreType.DMA((tiles,)),
        ],
        compiler_params=kernel_params(),
        name="prepare",
    )(picks, grads, error, accum)


def finish_kernel(
    order, own, hot, held, rows, grads, error, accum, _,
    error_out, accum_out, steps, errors, sums, sems,
):
    replica = lax.axis_index("rep")
    tiles = sems.shape[1]
    size = sums.shape[0] // tiles
    count = rows.shape[0] // SENT

    def split_rows():
        value = jnp.concatenate(
            [rows[pl.ds(j, count, SENT), :] for j in range(SENT)], axis=0
        )
        high = value.astype(jnp.bfloat16)
        low = (value - high.astype(jnp.float32)).astype(jnp.bfloat16)
        return jnp.concatenate([high, low], axis=1)

    def store_sum(tile, part, hot_tile, pair, base):
        both = jnp.dot(hot_tile, pair, preferred_element_type=jnp.float32)
        sums[part, :] = base + (both[:, :BLOCK] + both[:, BLOCK:])
        copy = pltpu.make_async_copy(
            sums.at[part, :], accum_out.at[part, :], sems.at[0, tile]
        )
        copy.start()
        return copy

    early = starts_early(replica)

    @pl.when(early)
    def _():
        pair = split_rows()
        stores = []
        first = 0
        for tile, size in enumerate(EARLY_TILES):
            part = pl.ds(first, size)
            first += size
            stores.append(store_sum(tile, part, hot[part, :], pair, held[part, :]))
        for store in stores:
            store.wait()

    @pl.when(jnp.logical_not(early))
    def _():
        def moves(tile):
            part = pl.ds(pl.multiple_of(tile * size, size), size)
            loads = (
                (accum.at[part, :], sums.at[part, :]),
                (grads.at[:, 0, part, :], steps.at[:, part, :]),
                (error.at[0, part, :], errors.at[part, :]),
            )
            stores = (
                (sums.at[part, :], accum_out.at[part, :]),
                (errors.at[part, :], error_out.at[0, part, :]),
            )
            made = [
                pltpu.make_async_copy(*pair, sems.at[place, tile])
                for place, pair in enumerate(loads + stores)
            ]
            return part, made[:3], made[3:]

        @pl.loop(0, tiles)
        def _(tile):
            for load in moves(tile)[1]:
                load.start()

        pair = split_rows()
        mine = [own[pl.ds(j, 1), :] for j in range(SENT)]

        @pl.loop(0, tiles)
        def _(tile):
            part, loads, stores = moves(tile)
            hot_tile = one_hot(order[...], tile * size, size)
            for load in loads:
                load.wait()
            both = jnp.dot(hot_tile, pair, preferred_element_type=jnp.float32)
            sums[part, :] += both[:, :BLOCK] + both[:, BLOCK:]
            step_tiles = [steps[step, part, :] for step in range(STEPS)]
            errors[part, :] = tile_error(step_tiles, errors[part, :], mine, tile * size)
            for store in stores:
                store.start()

        @pl.loop(0, tiles)
        def _(tile):
            for store in moves(tile)[2]:
                store.wait()


def finish(order, own, hot, held, rows, grads, error, accum, done, tiles=7):
    return pl.pallas_call(
        finish_kernel,
        out_shape=(
            pltpu.HBM(error.shape, jnp.float32),
            pltpu.HBM(accum.shape, jnp.float32),
        ),
        in_specs=[pl.BlockSpec(memory_space=pltpu.VMEM)] * 5
        + [pl.BlockSpec(memory_space=pltpu.HBM)] * 4,
        out_specs=(
            pl.BlockSpec(memory_space=pltpu.HBM),
            pl.BlockSpec(memory_space=pltpu.HBM),
        ),
        input_output_aliases={8: 0},
        scratch_shapes=[
            pltpu.VMEM((STEPS,) + accum.shape, jnp.bfloat16),
            pltpu.VMEM(accum.shape, jnp.float32),
            pltpu.VMEM(accum.shape, jnp.float32),
            pltpu.SemaphoreType.DMA((5, tiles)),
        ],
        compiler_params=kernel_params(),
        name="finish",
    )(order, own, hot, held, rows, grads, error, accum, done)


def exchange_order(count):
    return [(FIRST + place) % count for place in range(count)]


def local(grads, error_in, accum_in, picks):
    table = in_hbm(jnp.swapaxes(picks[:, :, 0, :], 1, 2))
    grads, error_in, accum_in = in_hbm(grads), in_hbm(error_in), in_hbm(accum_in)
    count = lax.axis_size("rep")
    members = exchange_order(count)
    rows, order, own, hot, held, done = prepare(table, grads, error_in, accum_in)
    rows = lax.all_to_all(
        rows, "rep", 0, 0, axis_index_groups=[members], tiled=True
    )
    rows = rows.reshape(count * SENT, BLOCK)
    error, accum = finish(
        order, own, hot, held, rows, grads, error_in, accum_in, in_hbm(done)
    )
    return (accum, error)


def solution(mesh):
    placed = (
        P(None, "rep", "tp", None),
        P("rep", "tp", None),
        P("tp", None),
        P(None, None, "tp", None),
    )
    return jax.shard_map(
        local,
        mesh=mesh,
        in_specs=placed,
        out_specs=(P("tp", None), P("rep", "tp", None)),
        check_vma=False,
    )
```
